32 devices in a mesh: wide: 8 (over z, x), narrow: 4 (over y, core).
Axes of the slice: x: 2, y: 2, z: 4, core: 2. Of those that a mesh axis runs over, the one named last changes fastest.
Arguments:
- amplitudes: float32 [16384, 1024], P('wide', 'narrow'), may hold values from -6 to 6
- ladder_blocks: float32 [128, 16, 128, 128], P('wide'), may hold values from -0.125 to 0.125
- ladder_index: int32 [128, 16], P('wide'), may hold values from 0 to 127, all different within a row
- cycle_blocks: float32 [32, 16, 128, 128], P(None, 'narrow'), may hold values from -0.125 to 0.125
- cycle_index: int32 [32, 16], P(None, 'narrow'), may hold values from 0 to 31, all different within a row
- eps_virt: float32 [128], replicated, may hold values from 0.3 to 1.5
- eps_occ: float32 [32], replicated, may hold values from -0.7 to -0.2
Outputs:
- new_amplitudes: float32 [16384, 1024], P('wide', 'narrow')
The draws below stay inside these ranges and needn't reach their ends.
Inputs may be any that keep to these rules, and one draw needn't show every extreme that they name: `ladder_index`: each row lists 16 different virtual indices, and every virtual index is listed by some row. `cycle_index`: each row lists 16 different occupied indices, and every occupied index is listed by some row.
All inputs are finite; a program needn't handle non-finite values.
Results may differ from the reference program's by a relative error of at most 0.000052.
Values sent between devices are 32-bit elements; how exact they have to be, the bound alone decides.
No kernel may reach another device: no remote copies, remote signals or barrier semaphores. Data moves between devices by JAX's collectives and lax.ppermute only.
A program may use at most 192 MiB of HBM per device.

```python
import jax
import jax.numpy as jnp
from jax import lax

V = 128
O = 32
LLIST = 16
RLIST = 16
PAIRS_V = 16384
PAIRS_O = 1024


def shard_levels(stream_key, extent, cuts, low, largest):
    level = 1.0
    for position, parts in cuts:
        heights = jax.random.uniform(jax.random.fold_in(jax.random.fold_in(stream_key, 6), position), (parts,), jnp.float32, low / len(cuts), largest / len(cuts))
        level = level * jnp.repeat(jnp.exp(heights), extent[position] // parts).reshape((-1,) + (1,) * (len(extent) - 1 - position))
    return level


def different_ones(own_key, rows, count, top, lift):
    sequence = jax.random.permutation(jax.random.fold_in(own_key, 1), count)
    boost = sequence
    for power in range(3):
        boost = boost * boost // count
    boost = boost * lift // count
    lots = jax.random.randint(jax.random.fold_in(own_key, 2), (rows, count), 0, 4096) + boost
    holders = jax.random.permutation(jax.random.fold_in(own_key, 3), rows)[jnp.arange(count) % rows]
    lots = jnp.where(jnp.arange(rows)[:, None] == holders[None, :], 1 << 14, lots)
    priority = lots * count + jnp.arange(count)
    return lax.top_k(priority.astype(jnp.int32), top)[1].astype(jnp.int32)


def gaussian(own_key, shape, scale, bound, shards=(), kind=jnp.bfloat16):
    entries = jax.random.normal(own_key, shape, jnp.float32) * scale
    if len(shards) > 0:
        entries = shard_levels(own_key, shape, shards, -0.22, 0.18) * entries
    return jnp.clip(entries, min=-bound, max=bound).astype(kind)


def setup_inputs(seed: int = 0) -> dict:
    arg_keys = jax.random.split(jax.random.key(seed), 8)
    amplitudes = gaussian(arg_keys[0], (PAIRS_V, PAIRS_O), 1.0, 6.0, ((0, 8), (1, 4)), jnp.float32)
    ladder_blocks = gaussian(arg_keys[1], (V, LLIST, V, V), (LLIST * V) ** -0.5, 0.125, ((0, 8),), jnp.float32)
    ladder_index = different_ones(arg_keys[2], V, V, LLIST, 0)
    cycle_blocks = gaussian(arg_keys[3], (O, RLIST, V, V), (RLIST * V) ** -0.5, 0.125, ((1, 4),), jnp.float32)
    cycle_index = different_ones(arg_keys[4], O, O, RLIST, 4096)
    eps_virt = jnp.clip(jax.random.uniform(arg_keys[5], (V,), jnp.float32, 0.3, 1.5), 0.3, 1.5)
    eps_occ = jnp.clip(jax.random.uniform(arg_keys[6], (O,), jnp.float32, -0.7, -0.2), -0.7, -0.2)
    return {"amplitudes": amplitudes, "ladder_blocks": ladder_blocks, "ladder_index": ladder_index, "cycle_blocks": cycle_blocks, "cycle_index": cycle_index, "eps_virt": eps_virt, "eps_occ": eps_occ}


def reference(amplitudes, ladder_blocks, ladder_index, cycle_blocks, cycle_index, eps_virt, eps_occ):
    by_virtual = amplitudes.reshape(V, V, O * O)

    def ladder_row(args):
        blocks, listed = args
        taken = by_virtual[listed]
        return jnp.einsum("kbd,kdn->bn", blocks, taken, precision=lax.Precision.HIGHEST)

    ladder = lax.map(ladder_row, (ladder_blocks, ladder_index)).reshape(V * V, O * O)
    amp_four = amplitudes.reshape(V, V, O, O)
    by_occupied = amp_four.transpose(2, 0, 1, 3).reshape(O, V, V * O)

    def cycle_row(args):
        blocks, listed = args
        taken = by_occupied[listed]
        return jnp.einsum("sac,scn->an", blocks, taken, precision=lax.Precision.HIGHEST)

    cycle_ph = lax.map(cycle_row, (cycle_blocks, cycle_index))
    cycle = cycle_ph.reshape(O, V, V, O).transpose(1, 2, 0, 3).reshape(V * V, O * O)
    denominator = (eps_virt[:, None, None, None] + eps_virt[None, :, None, None]
                   - eps_occ[None, None, :, None] - eps_occ[None, None, None, :])
    return (ladder + cycle) / denominator.reshape(V * V, O * O)
```

```python
import functools

import jax
import jax.numpy as jnp
from jax import lax
from jax.experimental import pallas as pl
from jax.experimental.pallas import tpu as pltpu
from jax.sharding import PartitionSpec as P

LANES = 128
PARTS = 4
F32 = jnp.float32
BF16 = jnp.bfloat16
ANY = pl.BlockSpec(memory_space=pl.ANY)
VMEM = pl.BlockSpec(memory_space=pltpu.VMEM)
SMEM = pl.BlockSpec(memory_space=pltpu.SMEM)


def params(mib, grid=0):
    semantics = ("arbitrary",) * grid if grid else None
    return pltpu.CompilerParams(vmem_limit_bytes=mib << 20, dimension_semantics=semantics)


def split(x):
    high = x.astype(BF16)
    return high, (x - high.astype(F32)).astype(BF16)


def dot(x, y):
    return jnp.dot(x, y, preferred_element_type=F32)


def swap_groups(arrays, group):
    arrays = list(arrays)
    count = len(arrays)
    lane = lax.broadcasted_iota(jnp.int32, arrays[0].shape, 1) // group
    bit = 1
    while bit < count:
        odd = (lane & bit) != 0
        for low in range(count):
            if low & bit:
                continue
            high = low | bit
            up = pltpu.roll(arrays[high], bit * group, 1)
            down = pltpu.roll(arrays[low], LANES - bit * group, 1)
            arrays[low], arrays[high] = (
                jnp.where(odd, up, arrays[low]),
                jnp.where(odd, arrays[high], down),
            )
        bit *= 2
    return arrays


def ladder_prep_kernel(blocks_ref, out_ref):
    slots, virt, _ = blocks_ref.shape[1:]
    parts = out_ref.shape[0]
    part = virt // parts
    per = LANES // part
    for first in range(0, slots, per):
        pieces = [blocks_ref[0, first + s] for s in range(per)]
        for q, piece in enumerate(swap_groups(pieces, part)):
            high, low = split(piece)
            lanes = pl.ds(first * part, LANES)
            out_ref[q, 0, 0:virt, lanes] = high
            out_ref[q, 0, virt : 2 * virt, lanes] = low


def ladder_prep(blocks, parts):
    a_here, slots, virt, _ = blocks.shape
    depth = slots * (virt // parts)
    return pl.pallas_call(
        ladder_prep_kernel,
        grid=(a_here,),
        in_specs=[pl.BlockSpec((1, slots, virt, virt), lambda a: (a, 0, 0, 0))],
        out_specs=pl.BlockSpec((parts, 1, 2 * virt, depth), lambda a: (0, a, 0, 0)),
        out_shape=jax.ShapeDtypeStruct((parts, a_here, 2 * virt, depth), BF16),
        compiler_params=params(24, 1),
        cost_estimate=pl.CostEstimate(
            flops=8 * blocks.size, bytes_accessed=8 * blocks.size, transcendentals=0
        ),
        name="ladder_prep",
    )(blocks)


def mirrored(rel, size):
    out = 0
    bit = 1
    while bit < size:
        out = out * 2 + (rel // bit) % 2
        bit *= 2
    return out


def cycle_prep_kernel(place_ref, index_ref, blocks_ref, high_ref, low_ref, dense):
    shares, occ, slots, a_here, virt = blocks_ref.shape
    i_here = occ // shares
    mine = place_ref[0]
    dense[...] = jnp.zeros_like(dense)
    for owner in range(shares):
        rel = mine ^ owner
        base = mirrored(rel, shares) * i_here

        @pl.loop(0, i_here)
        def _(i):
            for share in range(shares):
                for s in range(slots):
                    row = (share * occ + owner * i_here + i) * slots + s
                    k = index_ref[row] - mine * i_here

                    @pl.when((k >= 0) & (k < i_here))
                    def _():
                        lanes = pl.ds(pl.multiple_of(k * virt, virt), virt)
                        dense[base + i, :, lanes] = blocks_ref[share, owner * i_here + i, s]

    rows = occ * a_here
    step = i_here * a_here
    for first in range(shares):
        piece = dense[first * i_here : (first + 1) * i_here].reshape(step, i_here * virt)
        high, low = split(piece)
        high_ref[first * step : (first + 1) * step, :] = high
        low_ref[first * step : (first + 1) * step, :] = low


def cycle_prep(place, index, blocks):
    shares, occ, slots, a_here, virt = blocks.shape
    shape = jax.ShapeDtypeStruct((occ * a_here, occ // shares * virt), BF16)
    return pl.pallas_call(
        cycle_prep_kernel,
        in_specs=[SMEM, SMEM, VMEM],
        out_specs=[VMEM, VMEM],
        out_shape=[shape, shape],
        scratch_shapes=[pltpu.VMEM((occ, a_here, occ // shares * virt), F32)],
        compiler_params=params(24),
        cost_estimate=pl.CostEstimate(
            flops=2 * blocks.size, bytes_accessed=8 * blocks.size, transcendentals=0
        ),
        name="cycle_prep",
    )(place, index, blocks)


def fetch(source_ref, blocks, rows_each, held, sem):
    copies = []
    for n, (owner, offset, block) in enumerate(blocks):
        rows = block.shape[0]
        start = pl.multiple_of(source_ref[owner] * rows_each + offset, rows)
        for h in range(held.shape[0]):
            copies.append(
                pltpu.make_async_copy(
                    block.at[:, pl.ds(h * LANES, LANES)],
                    held.at[h, pl.ds(start, rows), :],
                    sem.at[n, h],
                )
            )
    for copy in copies:
        copy.start()
    return copies


def cycle_kernel(layout, part, occ, source_ref, *refs):
    count = len(layout)
    block_refs = refs[:count]
    high_ref, low_ref, keep_ref, send_ref, held, cols_high, cols_low, sem = refs[count:]
    halves, rows, _ = held.shape
    virt = rows // part
    rows_each = sum(n for o, _, n in layout if o == 0)
    blocks = [(o, f, r) for (o, f, _), r in zip(layout, block_refs)]
    for copy in fetch(source_ref, blocks, rows_each, held, sem):
        copy.wait()
    per = LANES // occ
    half_rows = keep_ref.shape[0]
    width = 2 * LANES
    steps = part // per

    for first in range(0, steps, 2):
        for g in range(first, first + 2):
            for h in range(halves):
                pieces = [held[h, pl.ds(g * per + m, virt, stride=part), :] for m in range(per)]
                for m, piece in enumerate(swap_groups(pieces, occ)):
                    k = h * per + m
                    high, low = split(piece)
                    lanes = pl.ds(g * LANES, LANES)
                    cols_high[k * virt : (k + 1) * virt, lanes] = high
                    cols_low[k * virt : (k + 1) * virt, lanes] = low
        lanes = pl.ds(first * LANES, width)
        right_high = cols_high[:, lanes]
        right_low = cols_low[:, lanes]
        for out_ref, top in ((send_ref, half_rows), (keep_ref, 0)):
            left_high = high_ref[top : top + half_rows, :]
            left_low = low_ref[top : top + half_rows, :]
            out_ref[:, lanes] = (
                dot(left_high, right_high) + dot(left_low, right_high) + dot(left_high, right_low)
            )


def cycle_part(layout, part, virt, occ, source, blocks, high, low):
    cols = blocks[0].shape[1]
    halves = cols // LANES
    rows, depth = high.shape
    wide = part * occ
    shape = jax.ShapeDtypeStruct((rows // 2, wide), F32)
    return pl.pallas_call(
        functools.partial(cycle_kernel, layout, part, occ),
        in_specs=[SMEM] + [ANY] * len(blocks) + [VMEM, VMEM],
        out_specs=[VMEM, VMEM],
        out_shape=[shape, shape],
        scratch_shapes=[
            pltpu.VMEM((halves, virt * part, LANES), F32),
            pltpu.VMEM((depth, wide), BF16),
            pltpu.VMEM((depth, wide), BF16),
            pltpu.SemaphoreType.DMA((len(blocks), halves)),
        ],
        compiler_params=params(40),
        cost_estimate=pl.CostEstimate(
            flops=6 * rows * depth * wide, bytes_accessed=4 * virt * part * cols, transcendentals=0
        ),
        name="cycle_part",
    )(source, *blocks, high, low)


def ladder_kernel(layout, part, again, source_ref, index_ref, *refs):
    count = len(layout)
    block_refs = refs[:count]
    left_ref = refs[count]
    before_ref = refs[count + 1] if again else None
    out_ref, held, right_high, right_low, sem = refs[count + 1 + again :]
    halves = held.shape[0]
    virt = out_ref.shape[1]
    slots = right_high.shape[0] // part
    a = pl.program_id(0)
    rows_each = sum(n for o, _, n in layout if o == 0)
    blocks = [(o, f, r) for (o, f, _), r in zip(layout, block_refs)]

    @pl.when(a == 0)
    def _():
        for copy in fetch(source_ref, blocks, rows_each, held, sem):
            copy.wait()

    for s in range(slots):
        start = pl.multiple_of(index_ref[a * slots + s] * part, part)
        for h in range(halves):
            high, low = split(held[h, pl.ds(start, part), :])
            right_high[s * part : (s + 1) * part, h * LANES : (h + 1) * LANES] = high
            right_low[s * part : (s + 1) * part, h * LANES : (h + 1) * LANES] = low
    both = dot(left_ref[0, 0], right_high[...])
    total = both[:virt] + both[virt:] + dot(left_ref[0, 0, :virt], right_low[...])
    if again:
        total = total + before_ref[0]
    out_ref[0] = total


def ladder_part(layout, part, q, source, index, blocks, left, before):
    cols = blocks[0].shape[1]
    halves = cols // LANES
    _, a_here, rows, depth = left.shape
    virt = rows // 2
    again = before is not None
    spec = pl.BlockSpec((1, virt, cols), lambda a, *_: (a, 0, 0))
    grid_spec = pltpu.PrefetchScalarGridSpec(
        num_scalar_prefetch=2,
        grid=(a_here,),
        in_specs=[ANY] * len(blocks)
        + [pl.BlockSpec((1, 1, rows, depth), lambda a, *_: (q, a, 0, 0))]
        + [spec] * again,
        out_specs=spec,
        scratch_shapes=[
            pltpu.VMEM((halves, virt * part, LANES), F32),
            pltpu.VMEM((depth, cols), BF16),
            pltpu.VMEM((depth, cols), BF16),
            pltpu.SemaphoreType.DMA((len(blocks), halves)),
        ],
    )
    aliases = {3 + len(blocks): 0} if again else {}
    return pl.pallas_call(
        functools.partial(ladder_kernel, layout, part, again),
        grid_spec=grid_spec,
        out_shape=jax.ShapeDtypeStruct((a_here, virt, cols), F32),
        input_output_aliases=aliases,
        compiler_params=params(24, 1),
        cost_estimate=pl.CostEstimate(
            flops=3 * a_here * rows * depth * cols,
            bytes_accessed=2 * left.size // left.shape[0],
            transcendentals=0,
        ),
        name="ladder_part",
    )(source, index, *blocks, left, *([before] if again else []))


def finish_kernel(parts, part, occ, virt_ref, *refs):
    energy_a, energy_ij, ladder_ref = refs[:3]
    terms = refs[3 : 3 + 3 * parts]
    out_ref = refs[3 + 3 * parts]
    a_here = energy_a.shape[0]
    halves, rows, _ = ladder_ref.shape
    virt = rows // a_here
    per = LANES // occ
    for q in range(parts):
        keep_ref, near_ref, far_ref = terms[3 * q : 3 * q + 3]

        @pl.loop(0, part // per)
        def _(g):
            lanes = pl.ds(pl.multiple_of(g * LANES, LANES), LANES)
            for h in range(halves):
                pieces = []
                for m in range(per):
                    here = pl.ds((h * per + m) * a_here, a_here)
                    pieces.append(keep_ref[here, lanes] + near_ref[here, lanes] + far_ref[here, lanes])
                for m, piece in enumerate(swap_groups(pieces, occ)):
                    b = q * part + g * per + m
                    here = pl.ds(b, a_here, stride=virt)
                    low = energy_a[...] + virt_ref[b] - energy_ij[h : h + 1, :]
                    out_ref[h, here, :] = (ladder_ref[h, here, :] + piece) / low


def finish(eps_virt, energy_a, energy_ij, ladder, terms, parts, part, occ):
    return None


def finish_body(parts, part, occ, virt_ref, energy_a, energy_ij, ladder_hbm, *refs):
    terms = refs[: 3 * parts]
    out_hbm, ladder_ref, out_ref, sem = refs[3 * parts :]
    halves = ladder_ref.shape[0]
    copies = [
        pltpu.make_async_copy(
            ladder_hbm.at[:, pl.ds(h * LANES, LANES)], ladder_ref.at[h], sem.at[h]
        )
        for h in range(halves)
    ]
    for copy in copies:
        copy.start()
    for copy in copies:
        copy.wait()
    finish_kernel(parts, part, occ, virt_ref, energy_a, energy_ij, ladder_ref, *terms, out_ref)
    copies = [
        pltpu.make_async_copy(out_ref.at[h], out_hbm.at[:, pl.ds(h * LANES, LANES)], sem.at[h])
        for h in range(halves)
    ]
    for copy in copies:
        copy.start()
    for copy in copies:
        copy.wait()


def finish_call(eps_virt, energy_a, energy_ij, ladder, terms, parts, part, occ):
    rows, cols = ladder.shape
    halves = cols // LANES
    return pl.pallas_call(
        functools.partial(finish_body, parts, part, occ),
        in_specs=[SMEM, VMEM, VMEM, ANY] + [VMEM] * len(terms),
        out_specs=ANY,
        out_shape=jax.ShapeDtypeStruct((rows, cols), F32),
        scratch_shapes=[
            pltpu.VMEM((halves, rows, LANES), F32),
            pltpu.VMEM((halves, rows, LANES), F32),
            pltpu.SemaphoreType.DMA((halves,)),
        ],
        compiler_params=params(32),
        name="finish",
    )(eps_virt, energy_a, energy_ij, ladder, *terms)


def ring_order(size):
    return list(range(0, size, 2)) + list(range(size - 1 - size % 2, 0, -2))


def per_device(
    amplitudes, ladder_blocks, ladder_index, cycle_blocks, cycle_index, eps_virt, eps_occ
):
    virt = eps_virt.shape[0]
    occ = eps_occ.shape[0]
    rows_here, cols = amplitudes.shape
    a_here = rows_here // virt
    i_here = cols // occ
    wide = lax.axis_size("wide")
    narrow = lax.axis_size("narrow")
    wide_pos = lax.axis_index("wide")
    narrow_pos = lax.axis_index("narrow")
    parts = PARTS
    part = virt // parts

    order = ring_order(wide)
    ahead = [(order[r], order[(r + 1) % wide]) for r in range(wide)]
    back = [(order[(r + 1) % wide], order[r]) for r in range(wide)]
    order_now = jnp.asarray(order, jnp.int32)
    spot = jnp.asarray([order.index(w) for w in range(wide)], jnp.int32)[wide_pos]
    steps = (wide - 1) // 2
    shifts = [0]
    for s in range(1, steps + 1):
        shifts += [-s, s]
    if wide % 2 == 0:
        shifts.append(wide // 2)
    source = order_now[(spot + jnp.asarray(shifts, jnp.int32)) % wide]

    own = amplitudes.reshape(a_here, virt, cols)
    rows_each = a_here * part

    place = narrow_pos.reshape(1).astype(jnp.int32)
    picked = lax.dynamic_slice_in_dim(cycle_blocks, wide_pos * a_here, a_here, 2)
    cycle_all = lax.all_gather(picked, "narrow", axis=0)
    index_all = lax.all_gather(cycle_index, "narrow", axis=0).reshape(-1)

    layout = None
    gathered = []
    for q in range(parts):
        block = own[:, q * part : (q + 1) * part, :].reshape(rows_each, cols)
        if q >= 2:
            block, _ = lax.optimization_barrier((block, gathered[q - 2][-3]))
        blocks = [block]
        layout = [(0, 0, rows_each)]
        right = left = block
        for s in range(steps):
            right = lax.ppermute(right, "wide", ahead)
            left = lax.ppermute(left, "wide", back)
            blocks += [right, left]
            layout += [(2 * s + 1, 0, rows_each), (2 * s + 2, 0, rows_each)]
        if wide % 2 == 0:
            half = rows_each // 2
            blocks.append(lax.ppermute(right[:half], "wide", ahead))
            blocks.append(lax.ppermute(left[half:], "wide", back))
            layout += [(wide - 1, 0, half), (wide - 1, half, rows_each - half)]
        gathered.append(blocks)

    left_all = ladder_prep(ladder_blocks, parts)
    dense_high, dense_low = cycle_prep(place, index_all, cycle_all)

    ladder = None
    terms = []
    ladder_list = ladder_index.reshape(-1)
    for q in range(parts):
        keep, send = cycle_part(layout, part, virt, occ, source, gathered[q], dense_high, dense_low)
        rows = keep.shape[0]
        near = lax.ppermute(send, "narrow", [(n, n ^ 1) for n in range(narrow)])
        pass_on = keep[rows // 2 :] + near[rows // 2 :]
        far = lax.ppermute(pass_on, "narrow", [(n, n ^ 2) for n in range(narrow)])
        terms += [keep, near, far]
        ladder = ladder_part(layout, part, q, source, ladder_list, gathered[q], left_all, ladder)

    energy_a = lax.dynamic_slice_in_dim(eps_virt, wide_pos * a_here, a_here, 0)
    energy_i = lax.dynamic_slice_in_dim(eps_occ, narrow_pos * i_here, i_here, 0)
    energy_ij = (energy_i[:, None] + eps_occ[None, :]).reshape(cols // LANES, LANES)
    energy_a = jnp.broadcast_to(energy_a[:, None], (a_here, LANES))
    return finish_call(
        eps_virt, energy_a, energy_ij, ladder.reshape(rows_here, cols), terms, parts, part, occ
    )


def solution(mesh):
    in_specs = (
        P("wide", "narrow"),
        P("wide", None, None, None),
        P("wide", None),
        P(None, "narrow", None, None),
        P(None, "narrow"),
        P(),
        P(),
    )
    out_specs = P("wide", "narrow")
    return jax.shard_map(
        per_device, mesh=mesh, in_specs=in_specs, out_specs=out_specs, check_vma=False
    )
```

```python
import functools

import jax
import jax.numpy as jnp
from jax import lax
from jax.experimental import pallas as pl
from jax.experimental.pallas import tpu as pltpu
from jax.sharding import PartitionSpec as P

LANES = 128
PARTS = 4
VMEM_MIB = 64


def cost(flops, moved):
    return pl.CostEstimate(flops=flops // 1000, bytes_accessed=moved // 1000, transcendentals=0)

F32 = jnp.float32
BF16 = jnp.bfloat16
HBM = pl.BlockSpec(memory_space=pltpu.HBM)
VMEM = pl.BlockSpec(memory_space=pltpu.VMEM)
SMEM = pl.BlockSpec(memory_space=pltpu.SMEM)


def params(mib):
    return pltpu.CompilerParams(vmem_limit_bytes=mib << 20)


def split(x):
    high = x.astype(BF16)
    return high, (x - high.astype(F32)).astype(BF16)


def dot(x, y):
    return jnp.dot(x, y, preferred_element_type=F32)


def swap_groups(arrays, group):
    arrays = list(arrays)
    count = len(arrays)
    lane = lax.broadcasted_iota(jnp.int32, arrays[0].shape, 1) // group
    bit = 1
    while bit < count:
        odd = (lane & bit) != 0
        for low in range(count):
            if low & bit:
                continue
            high = low | bit
            up = pltpu.roll(arrays[high], bit * group, 1)
            down = pltpu.roll(arrays[low], LANES - bit * group, 1)
            arrays[low], arrays[high] = (
                jnp.where(odd, up, arrays[low]),
                jnp.where(odd, arrays[high], down),
            )
        bit *= 2
    return arrays


def ladder_prep_kernel(blocks_ref, *refs):
    out_ref = refs[-1]
    slots, virt, _ = blocks_ref.shape[1:]
    parts = out_ref.shape[0]
    part = virt // parts
    per = LANES // part
    for first in range(0, slots, per):
        pieces = [blocks_ref[0, first + s] for s in range(per)]
        for q, piece in enumerate(swap_groups(pieces, part)):
            high, low = split(piece)
            lanes = pl.ds(first * part, LANES)
            out_ref[q, 0, 0:virt, lanes] = high
            out_ref[q, 0, virt : 2 * virt, lanes] = low


def ladder_prep(blocks, parts, first, count, before):
    a_here, slots, virt, _ = blocks.shape
    depth = slots * (virt // parts)
    again = before is not None
    spare = -(-(VMEM_MIB << 20) // (parts * a_here * 2 * virt * depth * 2))
    return pl.pallas_call(
        ladder_prep_kernel,
        grid=(count,),
        in_specs=[pl.BlockSpec((1, slots, virt, virt), lambda a: (first + a, 0, 0, 0))] + [HBM] * again,
        out_specs=pl.BlockSpec((parts, 1, 2 * virt, depth), lambda a: (0, first + a, 0, 0)),
        out_shape=jax.ShapeDtypeStruct(((1 + spare) * parts, a_here, 2 * virt, depth), BF16),
        input_output_aliases={1: 0} if again else {},
        compiler_params=params(12),
        cost_estimate=cost(8 * blocks.size * count // a_here, 8 * blocks.size * count // a_here),
        name="ladder_prep",
    )(blocks, *([before] if again else []))


def mirrored(rel, size):
    out = 0
    bit = 1
    while bit < size:
        out = out * 2 + (rel // bit) % 2
        bit *= 2
    return out


def cycle_prep_kernel(place_ref, index_ref, blocks_ref, high_ref, low_ref, dense):
    shares, occ, slots, a_here, virt = blocks_ref.shape
    i_here = occ // shares
    mine = place_ref[0]
    dense[...] = jnp.zeros_like(dense)
    for owner in range(shares):
        rel = mine ^ owner
        base = mirrored(rel, shares) * i_here

        @pl.loop(0, i_here)
        def _(i):
            for share in range(shares):
                for s in range(slots):
                    row = (share * occ + owner * i_here + i) * slots + s
                    k = index_ref[row] - mine * i_here

                    @pl.when((k >= 0) & (k < i_here))
                    def _():
                        lanes = pl.ds(pl.multiple_of(k * virt, virt), virt)
                        dense[base + i, :, lanes] = blocks_ref[share, owner * i_here + i, s]

    rows = occ * a_here
    step = i_here * a_here
    for first in range(shares):
        piece = dense[first * i_here : (first + 1) * i_here].reshape(step, i_here * virt)
        high, low = split(piece)
        high_ref[first * step : (first + 1) * step, :] = high
        low_ref[first * step : (first + 1) * step, :] = low


def cycle_prep(place, index, blocks):
    shares, occ, slots, a_here, virt = blocks.shape
    shape = jax.ShapeDtypeStruct((occ * a_here, occ // shares * virt), BF16)
    return pl.pallas_call(
        cycle_prep_kernel,
        in_specs=[SMEM, SMEM, VMEM],
        out_specs=[VMEM, VMEM],
        out_shape=[shape, shape],
        scratch_shapes=[pltpu.VMEM((occ, a_here, occ // shares * virt), F32)],
        compiler_params=params(12),
        cost_estimate=cost(2 * blocks.size, 8 * blocks.size),
        name="cycle_prep",
    )(place, index, blocks)


def place_blocks(layout, source_ref, block_refs, store):
    rows_each = layout[0][2]
    for (owner, offset, rows), block in zip(layout, block_refs):
        store(pl.multiple_of(source_ref[owner] * rows_each + offset, rows), rows, block)


def cycle_kernel(layout, part, occ, source_ref, *refs):
    count = len(layout)
    high_ref, low_ref, keep_ref, send_ref, held, cols_high, cols_low = refs[count:]
    halves, rows, _ = held.shape
    virt = rows // part

    def store(start, rows, block):
        @pl.loop(0, rows // part)
        def _(c):
            here = pl.ds(pl.multiple_of(c * part, part), part)
            there = pl.ds(pl.multiple_of(start + c * part, part), part)
            for h in range(halves):
                held[h, there, :] = block[here, h * LANES : (h + 1) * LANES]

    place_blocks(layout, source_ref, refs[:count], store)
    per = LANES // occ
    half_rows = keep_ref.shape[0]
    width = 2 * LANES
    steps = part // per

    for first in range(0, steps, 2):
        for g in range(first, first + 2):
            for h in range(halves):
                pieces = [held[h, pl.ds(g * per + m, virt, stride=part), :] for m in range(per)]
                for m, piece in enumerate(swap_groups(pieces, occ)):
                    k = h * per + m
                    high, low = split(piece)
                    lanes = pl.ds(g * LANES, LANES)
                    cols_high[k * virt : (k + 1) * virt, lanes] = high
                    cols_low[k * virt : (k + 1) * virt, lanes] = low
        lanes = pl.ds(first * LANES, width)
        right_high = cols_high[:, lanes]
        right_low = cols_low[:, lanes]
        for out_ref, top in ((send_ref, half_rows), (keep_ref, 0)):
            left_high = high_ref[top : top + half_rows, :]
            left_low = low_ref[top : top + half_rows, :]
            out_ref[:, lanes] = (
                dot(left_high, right_high) + dot(left_low, right_high) + dot(left_high, right_low)
            )


def cycle_part(layout, part, virt, occ, source, blocks, high, low):
    cols = blocks[0].shape[1]
    halves = cols // LANES
    rows, depth = high.shape
    wide = part * occ
    shape = jax.ShapeDtypeStruct((rows // 2, wide), F32)
    return pl.pallas_call(
        functools.partial(cycle_kernel, layout, part, occ),
        in_specs=[SMEM] + [VMEM] * len(blocks) + [VMEM, VMEM],
        out_specs=[VMEM, VMEM],
        out_shape=[shape, shape],
        scratch_shapes=[
            pltpu.VMEM((halves, virt * part, LANES), F32),
            pltpu.VMEM((depth, wide), BF16),
            pltpu.VMEM((depth, wide), BF16),
        ],
        compiler_params=params(18),
        cost_estimate=cost(6 * rows * depth * wide, 4 * virt * part * cols),
        name="cycle_part",
    )(source, *blocks, high, low)


def ladder_kernel(layout, part, q, again, last, source_ref, index_ref, *refs):
    count = len(layout)
    left_hbm = refs[count]
    before_ref = refs[count + 1] if again else None
    energies = refs[count + 1 + again : count + 1 + again + 3 * last]
    out_ref, left, held_high, held_low, right_high, right_low, sem = refs[
        count + 1 + again + 3 * last :
    ]
    a_here, virt, _ = out_ref.shape
    slots = right_high.shape[0] // part
    groups = sem.shape[0]
    each = a_here // groups
    copies = [
        pltpu.make_async_copy(
            left_hbm.at[q, pl.ds(n * each, each)], left.at[pl.ds(n * each, each)], sem.at[n]
        )
        for n in range(groups)
    ]
    for copy in copies:
        copy.start()

    def store(start, rows, block):
        @pl.loop(0, rows // part)
        def _(c):
            there = pl.ds(pl.multiple_of(start + c * part, part), part)
            high, low = split(block[pl.ds(pl.multiple_of(c * part, part), part), :])
            held_high[there, :] = high
            held_low[there, :] = low

    place_blocks(layout, source_ref, refs[:count], store)

    for n in range(groups):
        copies[n].wait()

        @pl.loop(n * each, (n + 1) * each)
        def _(a):
            for s in range(slots):
                rows = pl.ds(pl.multiple_of(index_ref[a * slots + s] * part, part), part)
                right_high[s * part : (s + 1) * part, :] = held_high[rows, :]
                right_low[s * part : (s + 1) * part, :] = held_low[rows, :]
            both = dot(left[a], right_high[...])
            total = both[:virt] + both[virt:] + dot(left[a, :virt], right_low[...])
            if again:
                total = total + before_ref[a]
            if last:
                energy_a, energy_b, energy_ij = energies
                low = (energy_a[pl.ds(a, 1), :] + energy_b[...]) - energy_ij[...]
                row = lax.broadcasted_iota(jnp.int32, total.shape, 0)
                total = jnp.where(row < virt - part, total / low, total)
            out_ref[a] = total


def ladder_part(layout, part, q, source, index, blocks, left, before, energies):
    cols = blocks[0].shape[1]
    _, a_here, rows, depth = left.shape
    virt = rows // 2
    again = before is not None
    last = len(energies) > 0
    return pl.pallas_call(
        functools.partial(ladder_kernel, layout, part, q, again, last),
        in_specs=[SMEM, SMEM] + [VMEM] * len(blocks) + [HBM] + [VMEM] * (again + len(energies)),
        out_specs=VMEM,
        out_shape=jax.ShapeDtypeStruct((a_here, virt, cols), F32),
        scratch_shapes=[
            pltpu.VMEM((a_here, rows, depth), BF16),
            pltpu.VMEM((virt * part, cols), BF16),
            pltpu.VMEM((virt * part, cols), BF16),
            pltpu.VMEM((depth, cols), BF16),
            pltpu.VMEM((depth, cols), BF16),
            pltpu.SemaphoreType.DMA((4,)),
        ],
        input_output_aliases={3 + len(blocks): 0} if again else {},
        compiler_params=params(18),
        cost_estimate=cost(3 * a_here * rows * depth * cols, 2 * left.size // left.shape[0]),
        name="ladder_part",
    )(source, index, *blocks, left, *([before] if again else []), *energies)


def join_kernel(q, part, occ, last, *refs):
    energy_a, energy_b, energy_ij, keep_ref, near_ref, far_ref, total_ref, out_ref, held = refs
    a_here, virt, cols = total_ref.shape
    halves = cols // LANES
    per = LANES // occ

    @pl.loop(0, part // per)
    def _(g):
        lanes = pl.ds(pl.multiple_of(g * LANES, LANES), LANES)
        for h in range(halves):
            pieces = []
            for m in range(per):
                here = pl.ds((h * per + m) * a_here, a_here)
                pieces.append(keep_ref[here, lanes] + near_ref[here, lanes] + far_ref[here, lanes])
            for m, piece in enumerate(swap_groups(pieces, occ)):
                held[h, pl.ds(g * per + m, a_here, stride=part), :] = piece

    @pl.loop(0, a_here)
    def _(a):
        for first in range(0, virt, part):
            rows = slice(first, first + part)
            total = total_ref[a, rows, :]
            if first == q * part:
                here = pl.ds(pl.multiple_of(a * part, part), part)
                total = total + jnp.concatenate([held[h, here, :] for h in range(halves)], axis=1)
                if last:
                    low = (energy_a[pl.ds(a, 1), :] + energy_b[rows, :]) - energy_ij[...]
                    total = total / low
            out_ref[a, rows, :] = total


def join(q, part, occ, last, energies, keep, near, far, total):
    a_here, _, cols = total.shape
    return pl.pallas_call(
        functools.partial(join_kernel, q, part, occ, last),
        in_specs=[VMEM] * (len(energies) + 4),
        out_specs=VMEM,
        out_shape=jax.ShapeDtypeStruct(total.shape, F32),
        scratch_shapes=[pltpu.VMEM((cols // LANES, a_here * part, LANES), F32)],
        input_output_aliases={len(energies) + 3: 0},
        compiler_params=params(18),
        cost_estimate=cost(8 * a_here * part * cols, 20 * a_here * part * cols),
        name="join",
    )(*energies, keep, near, far, total)


def ring_order(size):
    return list(range(0, size, 2)) + list(range(size - 1 - size % 2, 0, -2))


def per_device(
    amplitudes, ladder_blocks, ladder_index, cycle_blocks, cycle_index, eps_virt, eps_occ
):
    virt = eps_virt.shape[0]
    occ = eps_occ.shape[0]
    rows_here, cols = amplitudes.shape
    a_here = rows_here // virt
    i_here = cols // occ
    wide = lax.axis_size("wide")
    narrow = lax.axis_size("narrow")
    wide_pos = lax.axis_index("wide")
    narrow_pos = lax.axis_index("narrow")
    parts = PARTS
    part = virt // parts

    order = ring_order(wide)
    ahead = [(order[r], order[(r + 1) % wide]) for r in range(wide)]
    back = [(order[(r + 1) % wide], order[r]) for r in range(wide)]
    order_now = jnp.asarray(order, jnp.int32)
    spot = jnp.asarray([order.index(w) for w in range(wide)], jnp.int32)[wide_pos]
    steps = (wide - 1) // 2
    shifts = [0]
    for s in range(1, steps + 1):
        shifts += [-s, s]
    if wide % 2 == 0:
        shifts.append(wide // 2)
    source = order_now[(spot + jnp.asarray(shifts, jnp.int32)) % wide]

    own = amplitudes.reshape(a_here, virt, cols)
    rows_each = a_here * part

    hops = steps + (wide % 2 == 0)
    meet = hops // 2
    half = rows_each // 2
    layout = [(0, 0, rows_each)]
    for s in range(steps):
        layout += [(2 * s + 1, 0, rows_each), (2 * s + 2, 0, rows_each)]
    if wide % 2 == 0:
        layout += [(wide - 1, 0, half), (wide - 1, half, rows_each - half)]

    def tie(x, *others):
        return lax.optimization_barrier((x, *others))[0]

    ring = []
    for q in range(parts):
        whole = tie(own, ring[0][1]) if q else own
        block = whole[:, q * part : (q + 1) * part, :].reshape(rows_each, cols)
        ring.append([[block], block, block])

    token = []

    def ordered(x):
        return tie(x, *token) if token else x

    def hop(q, s, wait):
        blocks, right, left = ring[q]
        if wait:
            right, left, *_ = lax.optimization_barrier((right, left, *wait))
        if s == steps:
            right, left = right[:half], left[half:]
        right = lax.ppermute(right, "wide", ahead)
        left = lax.ppermute(left, "wide", back)
        blocks += [right, left]
        ring[q][1:] = [right, left]

    energy_a = lax.dynamic_slice_in_dim(eps_virt, wide_pos * a_here, a_here, 0)
    energy_i = lax.dynamic_slice_in_dim(eps_occ, narrow_pos * i_here, i_here, 0)
    energy_ij = (energy_i[:, None] + eps_occ[None, :]).reshape(1, cols)
    energies = [
        jnp.broadcast_to(energy_a[:, None], (a_here, cols)),
        jnp.broadcast_to(eps_virt[:, None], (virt, cols)),
        energy_ij,
    ]

    ladder_list = ladder_index.reshape(-1)
    keeps, nears, passes, fars = ([None] * parts for _ in range(4))
    total = None

    def cycle(q):
        blocks = [ordered(ring[q][0][0])] + ring[q][0][1:]
        keeps[q], send = cycle_part(layout, part, virt, occ, source, blocks, *dense)
        nears[q] = lax.ppermute(send, "narrow", [(n, n ^ 1) for n in range(narrow)])
        token[:] = [keeps[q]]

    def pass_on(q):
        keep = ordered(keeps[q])
        rows = keep.shape[0]
        passes[q] = keep[rows // 2 :] + nears[q][rows // 2 :]
        token[:] = [passes[q]]
        fars[q] = lax.ppermute(passes[q], "narrow", [(n, n ^ 2) for n in range(narrow)])

    def ladder(q, total):
        blocks = [ordered(ring[q][0][0])] + ring[q][0][1:]
        final = energies if q == parts - 1 else []
        total = ladder_part(
            layout, part, q, source, ladder_list, blocks, split_left, total, final
        )
        token[:] = [total]
        return total

    def add(q, total):
        last = q == parts - 1
        total = join(
            q, part, occ, last, energies, keeps[q], nears[q], fars[q], ordered(total)
        )
        token[:] = [total]
        return total

    def prepare(n, before):
        pieces = 4
        each = a_here // pieces
        out = ladder_prep(ordered(ladder_blocks), parts, n * each, each, before)
        token[:] = [out]
        return out

    walk = [[(0, s)] for s in range(meet)]
    for q in range(parts):
        rest = [(q, s) for s in range(meet, hops)]
        following = [(q + 1, s) for s in range(meet)] if q + 1 < parts else []
        for n in range(max(len(rest), len(following))):
            walk.append(rest[n : n + 1] + following[n : n + 1])
    whole_at = [max(n for n, step in enumerate(walk) if (q, hops - 1) in step) for q in range(parts)]

    last = parts - 1
    split_left = total = dense = None
    index_all = cycle_all = None
    place = narrow_pos.reshape(1).astype(jnp.int32)
    prepared = 0
    due = []
    for n, step in enumerate(walk):
        for q, s in step:
            hop(q, s, due)
        due = []
        if n == 0:
            index_all = lax.all_gather(cycle_index, "narrow", axis=0).reshape(-1)
            picked = lax.dynamic_slice_in_dim(
                tie(cycle_blocks, ring[0][0][0]), wide_pos * a_here, a_here, 2
            )
            cycle_all = lax.all_gather(picked, "narrow", axis=0)
        if prepared < 4:
            for _ in step:
                split_left = prepare(prepared, split_left)
                prepared += 1
        elif dense is None:
            dense = cycle_prep(place, ordered(index_all), cycle_all)
            token[:] = [dense[0]]
        for q in range(last):
            if n == whole_at[q] + 1:
                cycle(q)
            if n == whole_at[q] + 2:
                if q < last - 1:
                    total = ladder(q, total)
                pass_on(q)
            if n == whole_at[q] + 3:
                due.append(fars[q])
        due += token
    total = ladder(last - 1, total)
    cycle(last)
    for q in range(last - 1):
        total = add(q, total)
    token.append(fars[last - 1])
    pass_on(last)
    total = add(last - 1, total)
    total = ladder(last, total)
    total = add(last, total)
    return total.reshape(rows_here, cols)


def solution(mesh):
    in_specs = (
        P("wide", "narrow"),
        P("wide", None, None, None),
        P("wide", None),
        P(None, "narrow", None, None),
        P(None, "narrow"),
        P(),
        P(),
    )
    out_specs = P("wide", "narrow")
    return jax.shard_map(
        per_device, mesh=mesh, in_specs=in_specs, out_specs=out_specs, check_vma=False
    )
```

```python
import functools

import jax
import jax.numpy as jnp
from jax import lax
from jax.experimental import pallas as pl
from jax.experimental.pallas import tpu as pltpu
from jax.sharding import PartitionSpec as P

LANES = 128
PARTS = 4
VMEM_MIB = 64


def cost(flops, moved):
    return pl.CostEstimate(flops=flops // 1000, bytes_accessed=moved // 1000, transcendentals=0)

F32 = jnp.float32
BF16 = jnp.bfloat16
HBM = pl.BlockSpec(memory_space=pltpu.HBM)
VMEM = pl.BlockSpec(memory_space=pltpu.VMEM)
SMEM = pl.BlockSpec(memory_space=pltpu.SMEM)


def params(mib):
    return pltpu.CompilerParams(vmem_limit_bytes=mib << 20)


def split(x):
    high = x.astype(BF16)
    return high, (x - high.astype(F32)).astype(BF16)


def dot(x, y):
    return jnp.dot(x, y, preferred_element_type=F32)


def swap_groups(arrays, group):
    arrays = list(arrays)
    count = len(arrays)
    lane = lax.broadcasted_iota(jnp.int32, arrays[0].shape, 1) // group
    bit = 1
    while bit < count:
        odd = (lane & bit) != 0
        for low in range(count):
            if low & bit:
                continue
            high = low | bit
            up = pltpu.roll(arrays[high], bit * group, 1)
            down = pltpu.roll(arrays[low], LANES - bit * group, 1)
            arrays[low], arrays[high] = (
                jnp.where(odd, up, arrays[low]),
                jnp.where(odd, arrays[high], down),
            )
        bit *= 2
    return arrays


def ladder_prep_kernel(blocks_ref, *refs):
    out_ref = refs[-1]
    slots, virt, _ = blocks_ref.shape[1:]
    parts = out_ref.shape[0]
    part = virt // parts
    per = LANES // part
    for first in range(0, slots, per):
        pieces = [blocks_ref[0, first + s] for s in range(per)]
        for q, piece in enumerate(swap_groups(pieces, part)):
            high, low = split(piece)
            lanes = pl.ds(first * part, LANES)
            out_ref[q, 0, 0:virt, lanes] = high
            out_ref[q, 0, virt : 2 * virt, lanes] = low


def ladder_prep(blocks, parts, first, count, before):
    a_here, slots, virt, _ = blocks.shape
    depth = slots * (virt // parts)
    again = before is not None
    spare = -(-(VMEM_MIB << 20) // (parts * a_here * 2 * virt * depth * 2))
    return pl.pallas_call(
        ladder_prep_kernel,
        grid=(count,),
        in_specs=[pl.BlockSpec((1, slots, virt, virt), lambda a: (first + a, 0, 0, 0))] + [HBM] * again,
        out_specs=pl.BlockSpec((parts, 1, 2 * virt, depth), lambda a: (0, first + a, 0, 0)),
        out_shape=jax.ShapeDtypeStruct(((1 + spare) * parts, a_here, 2 * virt, depth), BF16),
        input_output_aliases={1: 0} if again else {},
        compiler_params=params(12),
        cost_estimate=cost(8 * blocks.size * count // a_here, 8 * blocks.size * count // a_here),
        name="ladder_prep",
    )(blocks, *([before] if again else []))


def mirrored(rel, size):
    out = 0
    bit = 1
    while bit < size:
        out = out * 2 + (rel // bit) % 2
        bit *= 2
    return out


def cycle_prep_kernel(place_ref, index_ref, blocks_ref, high_ref, low_ref, dense):
    shares, occ, slots, a_here, virt = blocks_ref.shape
    i_here = occ // shares
    mine = place_ref[0]
    dense[...] = jnp.zeros_like(dense)
    for owner in range(shares):
        rel = mine ^ owner
        base = mirrored(rel, shares) * i_here

        @pl.loop(0, i_here)
        def _(i):
            for share in range(shares):
                for s in range(slots):
                    row = (share * occ + owner * i_here + i) * slots + s
                    k = index_ref[row] - mine * i_here

                    @pl.when((k >= 0) & (k < i_here))
                    def _():
                        lanes = pl.ds(pl.multiple_of(k * virt, virt), virt)
                        dense[base + i, :, lanes] = blocks_ref[share, owner * i_here + i, s]

    rows = occ * a_here
    step = i_here * a_here
    for first in range(shares):
        piece = dense[first * i_here : (first + 1) * i_here].reshape(step, i_here * virt)
        high, low = split(piece)
        high_ref[first * step : (first + 1) * step, :] = high
        low_ref[first * step : (first + 1) * step, :] = low


def cycle_prep(place, index, blocks):
    shares, occ, slots, a_here, virt = blocks.shape
    shape = jax.ShapeDtypeStruct((occ * a_here, occ // shares * virt), BF16)
    return pl.pallas_call(
        cycle_prep_kernel,
        in_specs=[SMEM, SMEM, VMEM],
        out_specs=[VMEM, VMEM],
        out_shape=[shape, shape],
        scratch_shapes=[pltpu.VMEM((occ, a_here, occ // shares * virt), F32)],
        compiler_params=params(12),
        cost_estimate=cost(2 * blocks.size, 8 * blocks.size),
        name="cycle_prep",
    )(place, index, blocks)


def place_blocks(layout, source_ref, block_refs, store):
    rows_each = layout[0][2]
    for (owner, offset, rows), block in zip(layout, block_refs):
        store(pl.multiple_of(source_ref[owner] * rows_each + offset, rows), rows, block)


def cycle_kernel(layout, part, occ, source_ref, *refs):
    count = len(layout)
    high_ref, low_ref, keep_ref, send_ref, held, cols_high, cols_low = refs[count:]
    halves, rows, _ = held.shape
    virt = rows // part

    def store(start, rows, block):
        @pl.loop(0, rows // part)
        def _(c):
            here = pl.ds(pl.multiple_of(c * part, part), part)
            there = pl.ds(pl.multiple_of(start + c * part, part), part)
            for h in range(halves):
                held[h, there, :] = block[here, h * LANES : (h + 1) * LANES]

    place_blocks(layout, source_ref, refs[:count], store)
    per = LANES // occ
    half_rows = keep_ref.shape[0]
    width = 2 * LANES
    steps = part // per

    for first in range(0, steps, 2):
        for g in range(first, first + 2):
            for h in range(halves):
                pieces = [held[h, pl.ds(g * per + m, virt, stride=part), :] for m in range(per)]
                for m, piece in enumerate(swap_groups(pieces, occ)):
                    k = h * per + m
                    high, low = split(piece)
                    lanes = pl.ds(g * LANES, LANES)
                    cols_high[k * virt : (k + 1) * virt, lanes] = high
                    cols_low[k * virt : (k + 1) * virt, lanes] = low
        lanes = pl.ds(first * LANES, width)
        right_high = cols_high[:, lanes]
        right_low = cols_low[:, lanes]
        for out_ref, top in ((send_ref, half_rows), (keep_ref, 0)):
            left_high = high_ref[top : top + half_rows, :]
            left_low = low_ref[top : top + half_rows, :]
            out_ref[:, lanes] = (
                dot(left_high, right_high) + dot(left_low, right_high) + dot(left_high, right_low)
            )


def cycle_part(layout, part, virt, occ, source, blocks, high, low):
    cols = blocks[0].shape[1]
    halves = cols // LANES
    rows, depth = high.shape
    wide = part * occ
    shape = jax.ShapeDtypeStruct((rows // 2, wide), F32)
    return pl.pallas_call(
        functools.partial(cycle_kernel, layout, part, occ),
        in_specs=[SMEM] + [VMEM] * len(blocks) + [VMEM, VMEM],
        out_specs=[VMEM, VMEM],
        out_shape=[shape, shape],
        scratch_shapes=[
            pltpu.VMEM((halves, virt * part, LANES), F32),
            pltpu.VMEM((depth, wide), BF16),
            pltpu.VMEM((depth, wide), BF16),
        ],
        compiler_params=params(18),
        cost_estimate=cost(6 * rows * depth * wide, 4 * virt * part * cols),
        name="cycle_part",
    )(source, *blocks, high, low)


def ladder_kernel(layout, part, q, again, source_ref, index_ref, *refs):
    count = len(layout)
    left_hbm = refs[count]
    before_ref = refs[count + 1] if again else None
    out_ref, left, held_high, held_low, right_high, right_low, sem = refs[count + 1 + again :]
    a_here, virt, _ = out_ref.shape
    slots = right_high.shape[1] // part
    groups = sem.shape[0]
    each = a_here // groups
    copies = [
        pltpu.make_async_copy(
            left_hbm.at[q, pl.ds(n * each, each)], left.at[pl.ds(n * each, each)], sem.at[n]
        )
        for n in range(groups)
    ]
    for copy in copies:
        copy.start()

    def store(start, rows, block):
        @pl.loop(0, rows // part)
        def _(c):
            there = pl.ds(pl.multiple_of(start + c * part, part), part)
            high, low = split(block[pl.ds(pl.multiple_of(c * part, part), part), :])
            held_high[there, :] = high
            held_low[there, :] = low

    place_blocks(layout, source_ref, refs[:count], store)

    for n in range(groups):
        copies[n].wait()

        for a in range(n * each, (n + 1) * each):
            turn = a % 2
            for s in range(slots):
                rows = pl.ds(pl.multiple_of(index_ref[a * slots + s] * part, part), part)
                right_high[turn, s * part : (s + 1) * part, :] = held_high[rows, :]
                right_low[turn, s * part : (s + 1) * part, :] = held_low[rows, :]
            both = dot(left[a], right_high[turn])
            total = both[:virt] + both[virt:] + dot(left[a, :virt], right_low[turn])
            if again:
                total = total + before_ref[a]
            out_ref[a] = total


def ladder_part(layout, part, q, source, index, blocks, left, before):
    cols = blocks[0].shape[1]
    _, a_here, rows, depth = left.shape
    virt = rows // 2
    again = before is not None
    return pl.pallas_call(
        functools.partial(ladder_kernel, layout, part, q, again),
        in_specs=[SMEM, SMEM] + [VMEM] * len(blocks) + [HBM] + [VMEM] * again,
        out_specs=VMEM,
        out_shape=jax.ShapeDtypeStruct((a_here, virt, cols), F32),
        scratch_shapes=[
            pltpu.VMEM((a_here, rows, depth), BF16),
            pltpu.VMEM((virt * part, cols), BF16),
            pltpu.VMEM((virt * part, cols), BF16),
            pltpu.VMEM((2, depth, cols), BF16),
            pltpu.VMEM((2, depth, cols), BF16),
            pltpu.SemaphoreType.DMA((4,)),
        ],
        input_output_aliases={3 + len(blocks): 0} if again else {},
        compiler_params=params(18),
        cost_estimate=cost(3 * a_here * rows * depth * cols, 2 * left.size // left.shape[0]),
        name="ladder_part",
    )(source, index, *blocks, left, *([before] if again else []))


def join_kernel(parts, part, occ, over, *refs):
    energies, terms = refs[:3], refs[3 : 3 + 3 * len(parts)]
    total_ref, out_ref, held = refs[3 + 3 * len(parts) :]
    energy_a, energy_b, energy_ij = energies
    a_here, virt, cols = total_ref.shape
    halves = cols // LANES
    per = LANES // occ

    @pl.loop(0, part // per)
    def _(g):
        lanes = pl.ds(pl.multiple_of(g * LANES, LANES), LANES)
        for n in range(len(parts)):
            keep_ref, near_ref, far_ref = terms[3 * n : 3 * n + 3]
            for h in range(halves):
                pieces = []
                for m in range(per):
                    here = pl.ds((h * per + m) * a_here, a_here)
                    pieces.append(
                        keep_ref[here, lanes] + near_ref[here, lanes] + far_ref[here, lanes]
                    )
                for m, piece in enumerate(swap_groups(pieces, occ)):
                    held[n, h, pl.ds(g * per + m, a_here, stride=part), :] = piece

    @pl.loop(0, a_here)
    def _(a):
        for q in range(virt // part):
            rows = slice(q * part, (q + 1) * part)
            total = total_ref[a, rows, :]
            if q in parts:
                n = parts.index(q)
                here = pl.ds(pl.multiple_of(a * part, part), part)
                total = total + jnp.concatenate([held[n, h, here, :] for h in range(halves)], axis=1)
            if q in over:
                low = (energy_a[pl.ds(a, 1), :] + energy_b[rows, :]) - energy_ij[...]
                total = total / low
            out_ref[a, rows, :] = total


def join(parts, part, occ, over, energies, terms, total):
    a_here, _, cols = total.shape
    return pl.pallas_call(
        functools.partial(join_kernel, parts, part, occ, over),
        in_specs=[VMEM] * (len(energies) + len(terms) + 1),
        out_specs=VMEM,
        out_shape=jax.ShapeDtypeStruct(total.shape, F32),
        scratch_shapes=[pltpu.VMEM((len(parts), cols // LANES, a_here * part, LANES), F32)],
        input_output_aliases={len(energies) + len(terms): 0},
        compiler_params=params(18),
        cost_estimate=cost(8 * a_here * part * cols, 20 * a_here * part * cols),
        name="join",
    )(*energies, *terms, total)


def ring_order(size):
    return list(range(0, size, 2)) + list(range(size - 1 - size % 2, 0, -2))


def per_device(
    amplitudes, ladder_blocks, ladder_index, cycle_blocks, cycle_index, eps_virt, eps_occ
):
    virt = eps_virt.shape[0]
    occ = eps_occ.shape[0]
    rows_here, cols = amplitudes.shape
    a_here = rows_here // virt
    i_here = cols // occ
    wide = lax.axis_size("wide")
    narrow = lax.axis_size("narrow")
    wide_pos = lax.axis_index("wide")
    narrow_pos = lax.axis_index("narrow")
    parts = PARTS
    part = virt // parts

    order = ring_order(wide)
    ahead = [(order[r], order[(r + 1) % wide]) for r in range(wide)]
    back = [(order[(r + 1) % wide], order[r]) for r in range(wide)]
    order_now = jnp.asarray(order, jnp.int32)
    spot = jnp.asarray([order.index(w) for w in range(wide)], jnp.int32)[wide_pos]
    steps = (wide - 1) // 2
    shifts = [0]
    for s in range(1, steps + 1):
        shifts += [-s, s]
    if wide % 2 == 0:
        shifts.append(wide // 2)
    source = order_now[(spot + jnp.asarray(shifts, jnp.int32)) % wide]

    own = amplitudes.reshape(a_here, virt, cols)
    rows_each = a_here * part

    hops = steps + (wide % 2 == 0)
    meet = hops // 2
    half = rows_each // 2
    layout = [(0, 0, rows_each)]
    for s in range(steps):
        layout += [(2 * s + 1, 0, rows_each), (2 * s + 2, 0, rows_each)]
    if wide % 2 == 0:
        layout += [(wide - 1, 0, half), (wide - 1, half, rows_each - half)]

    def tie(x, *others):
        return lax.optimization_barrier((x, *others))[0]

    ring = []
    for q in range(parts):
        whole = tie(own, ring[0][1]) if q else own
        block = whole[:, q * part : (q + 1) * part, :].reshape(rows_each, cols)
        ring.append([[block], block, block])

    token = []

    def ordered(x):
        return tie(x, *token) if token else x

    def hop(q, s, wait):
        blocks, right, left = ring[q]
        if wait:
            right, left, *_ = lax.optimization_barrier((right, left, *wait))
        if s == steps:
            right, left = right[:half], left[half:]
        right = lax.ppermute(right, "wide", ahead)
        left = lax.ppermute(left, "wide", back)
        blocks += [right, left]
        ring[q][1:] = [right, left]

    energy_a = lax.dynamic_slice_in_dim(eps_virt, wide_pos * a_here, a_here, 0)
    energy_i = lax.dynamic_slice_in_dim(eps_occ, narrow_pos * i_here, i_here, 0)
    energy_ij = (energy_i[:, None] + eps_occ[None, :]).reshape(1, cols)
    energies = [
        jnp.broadcast_to(energy_a[:, None], (a_here, cols)),
        jnp.broadcast_to(eps_virt[:, None], (virt, cols)),
        energy_ij,
    ]

    ladder_list = ladder_index.reshape(-1)
    keeps, nears, passes, fars = ([None] * parts for _ in range(4))
    total = None

    def cycle(q):
        blocks = [ordered(ring[q][0][0])] + ring[q][0][1:]
        keeps[q], send = cycle_part(layout, part, virt, occ, source, blocks, *dense)
        nears[q] = lax.ppermute(send, "narrow", [(n, n ^ 1) for n in range(narrow)])
        token[:] = [keeps[q]]

    def pass_on(q):
        keep = ordered(keeps[q])
        rows = keep.shape[0]
        passes[q] = keep[rows // 2 :] + nears[q][rows // 2 :]
        token[:] = [passes[q]]
        fars[q] = lax.ppermute(passes[q], "narrow", [(n, n ^ 2) for n in range(narrow)])

    def ladder(q, total):
        blocks = [ordered(ring[q][0][0])] + ring[q][0][1:]
        total = ladder_part(layout, part, q, source, ladder_list, blocks, split_left, total)
        token[:] = [total]
        return total

    def add(which, over, total):
        terms = [x for q in which for x in (keeps[q], nears[q], fars[q])]
        total = join(which, part, occ, over, energies, terms, ordered(total))
        token[:] = [total]
        return total

    def prepare(n, before):
        pieces = 4
        each = a_here // pieces
        out = ladder_prep(ordered(ladder_blocks), parts, n * each, each, before)
        token[:] = [out]
        return out

    walk = [[(0, s)] for s in range(meet)]
    for q in range(parts):
        rest = [(q, s) for s in range(meet, hops)]
        following = [(q + 1, s) for s in range(meet)] if q + 1 < parts else []
        for n in range(max(len(rest), len(following))):
            walk.append(rest[n : n + 1] + following[n : n + 1])
    whole_at = [max(n for n, step in enumerate(walk) if (q, hops - 1) in step) for q in range(parts)]

    last = parts - 1
    split_left = total = dense = None
    index_all = cycle_all = None
    place = narrow_pos.reshape(1).astype(jnp.int32)
    prepared = 0
    due = []
    for n, step in enumerate(walk):
        before = ring[step[0][0]][1:]
        for q, s in step:
            hop(q, s, due)
        due = []
        if n == 0:
            index_all = lax.all_gather(cycle_index, "narrow", axis=0).reshape(-1)
            picked = lax.dynamic_slice_in_dim(
                tie(cycle_blocks, ring[0][0][0]), wide_pos * a_here, a_here, 2
            )
            cycle_all = lax.all_gather(picked, "narrow", axis=0)
        if prepared < 4:
            for _ in step:
                split_left = prepare(prepared, split_left)
                prepared += 1
        elif dense is None:
            dense = cycle_prep(place, ordered(index_all), cycle_all)
            token[:] = [dense[0]]
        for q in range(last):
            if n == whole_at[q] + 1:
                if len(step) == 1:
                    token += before
                cycle(q)
            if n == whole_at[q] + 2:
                if q < last - 1:
                    total = ladder(q, total)
                pass_on(q)
            if n == whole_at[q] + 3:
                due.append(fars[q])
        due += token
    total = ladder(last - 1, total)
    token.append(fars[last - 1])
    cycle(last)
    pass_on(last)
    total = ladder(last, total)
    total = add(list(range(last)), list(range(last)), total)
    total = add([last], [last], total)
    return total.reshape(rows_here, cols)


def solution(mesh):
    in_specs = (
        P("wide", "narrow"),
        P("wide", None, None, None),
        P("wide", None),
        P(None, "narrow", None, None),
        P(None, "narrow"),
        P(),
        P(),
    )
    out_specs = P("wide", "narrow")
    return jax.shard_map(
        per_device, mesh=mesh, in_specs=in_specs, out_specs=out_specs, check_vma=False
    )
```

```python
import functools

import jax
import jax.numpy as jnp
from jax import lax
from jax.experimental import pallas as pl
from jax.experimental.pallas import tpu as pltpu
from jax.sharding import PartitionSpec as P

LANES = 128
PARTS = 4
VMEM_MIB = 64


def cost(flops, moved):
    return pl.CostEstimate(flops=flops // 1000, bytes_accessed=moved // 1000, transcendentals=0)

F32 = jnp.float32
BF16 = jnp.bfloat16
HBM = pl.BlockSpec(memory_space=pltpu.HBM)
VMEM = pl.BlockSpec(memory_space=pltpu.VMEM)
SMEM = pl.BlockSpec(memory_space=pltpu.SMEM)


def params(mib):
    return pltpu.CompilerParams(vmem_limit_bytes=mib << 20)


def split(x):
    high = x.astype(BF16)
    return high, (x - high.astype(F32)).astype(BF16)


def dot(x, y):
    return jnp.dot(x, y, preferred_element_type=F32)


def swap_groups(arrays, group):
    arrays = list(arrays)
    count = len(arrays)
    lane = lax.broadcasted_iota(jnp.int32, arrays[0].shape, 1) // group
    bit = 1
    while bit < count:
        odd = (lane & bit) != 0
        for low in range(count):
            if low & bit:
                continue
            high = low | bit
            up = pltpu.roll(arrays[high], bit * group, 1)
            down = pltpu.roll(arrays[low], LANES - bit * group, 1)
            arrays[low], arrays[high] = (
                jnp.where(odd, up, arrays[low]),
                jnp.where(odd, arrays[high], down),
            )
        bit *= 2
    return arrays


def ladder_prep_kernel(blocks_ref, *refs):
    out_ref = refs[-1]
    slots, virt, _ = blocks_ref.shape[1:]
    parts = out_ref.shape[0]
    part = virt // parts
    per = LANES // part
    for first in range(0, slots, per):
        pieces = [blocks_ref[0, first + s] for s in range(per)]
        for q, piece in enumerate(swap_groups(pieces, part)):
            high, low = split(piece)
            lanes = pl.ds(first * part, LANES)
            out_ref[q, 0, 0:virt, lanes] = high
            out_ref[q, 0, virt : 2 * virt, lanes] = low


def ladder_prep(blocks, parts, first, count, before):
    a_here, slots, virt, _ = blocks.shape
    depth = slots * (virt // parts)
    again = before is not None
    spare = -(-(VMEM_MIB << 20) // (parts * a_here * 2 * virt * depth * 2))
    return pl.pallas_call(
        ladder_prep_kernel,
        grid=(count,),
        in_specs=[pl.BlockSpec((1, slots, virt, virt), lambda a: (first + a, 0, 0, 0))] + [HBM] * again,
        out_specs=pl.BlockSpec((parts, 1, 2 * virt, depth), lambda a: (0, first + a, 0, 0)),
        out_shape=jax.ShapeDtypeStruct(((1 + spare) * parts, a_here, 2 * virt, depth), BF16),
        input_output_aliases={1: 0} if again else {},
        compiler_params=params(12),
        cost_estimate=cost(8 * blocks.size * count // a_here, 8 * blocks.size * count // a_here),
        name="ladder_prep",
    )(blocks, *([before] if again else []))


def mirrored(rel, size):
    out = 0
    bit = 1
    while bit < size:
        out = out * 2 + (rel // bit) % 2
        bit *= 2
    return out


def cycle_prep_kernel(place_ref, index_ref, blocks_ref, high_ref, low_ref, dense):
    shares, occ, slots, a_here, virt = blocks_ref.shape
    i_here = occ // shares
    mine = place_ref[0]
    dense[...] = jnp.zeros_like(dense)
    for owner in range(shares):
        rel = mine ^ owner
        base = mirrored(rel, shares) * i_here

        @pl.loop(0, i_here)
        def _(i):
            for share in range(shares):
                for s in range(slots):
                    row = (share * occ + owner * i_here + i) * slots + s
                    k = index_ref[row] - mine * i_here

                    @pl.when((k >= 0) & (k < i_here))
                    def _():
                        lanes = pl.ds(pl.multiple_of(k * virt, virt), virt)
                        dense[base + i, :, lanes] = blocks_ref[share, owner * i_here + i, s]

    rows = occ * a_here
    step = i_here * a_here
    for first in range(shares):
        piece = dense[first * i_here : (first + 1) * i_here].reshape(step, i_here * virt)
        high, low = split(piece)
        high_ref[first * step : (first + 1) * step, :] = high
        low_ref[first * step : (first + 1) * step, :] = low


def cycle_prep(place, index, blocks):
    shares, occ, slots, a_here, virt = blocks.shape
    shape = jax.ShapeDtypeStruct((occ * a_here, occ // shares * virt), BF16)
    return pl.pallas_call(
        cycle_prep_kernel,
        in_specs=[SMEM, SMEM, VMEM],
        out_specs=[VMEM, VMEM],
        out_shape=[shape, shape],
        scratch_shapes=[pltpu.VMEM((occ, a_here, occ // shares * virt), F32)],
        compiler_params=params(12),
        cost_estimate=cost(2 * blocks.size, 8 * blocks.size),
        name="cycle_prep",
    )(place, index, blocks)


def place_blocks(layout, source_ref, block_refs, store):
    rows_each = layout[0][2]
    for (owner, offset, rows), block in zip(layout, block_refs):
        store(pl.multiple_of(source_ref[owner] * rows_each + offset, rows), rows, block)


def cycle_kernel(layout, part, occ, source_ref, *refs):
    count = len(layout)
    high_ref, low_ref, keep_ref, send_ref, held, cols_high, cols_low = refs[count:]
    halves, rows, _ = held.shape
    virt = rows // part

    def store(start, rows, block):
        @pl.loop(0, rows // part)
        def _(c):
            here = pl.ds(pl.multiple_of(c * part, part), part)
            there = pl.ds(pl.multiple_of(start + c * part, part), part)
            for h in range(halves):
                held[h, there, :] = block[here, h * LANES : (h + 1) * LANES]

    place_blocks(layout, source_ref, refs[:count], store)
    per = LANES // occ
    half_rows = keep_ref.shape[0]
    width = 2 * LANES
    steps = part // per

    for first in range(0, steps, 2):
        for g in range(first, first + 2):
            for h in range(halves):
                pieces = [held[h, pl.ds(g * per + m, virt, stride=part), :] for m in range(per)]
                for m, piece in enumerate(swap_groups(pieces, occ)):
                    k = h * per + m
                    high, low = split(piece)
                    lanes = pl.ds(g * LANES, LANES)
                    cols_high[k * virt : (k + 1) * virt, lanes] = high
                    cols_low[k * virt : (k + 1) * virt, lanes] = low
        lanes = pl.ds(first * LANES, width)
        right_high = cols_high[:, lanes]
        right_low = cols_low[:, lanes]
        for out_ref, top in ((send_ref, half_rows), (keep_ref, 0)):
            left_high = high_ref[top : top + half_rows, :]
            left_low = low_ref[top : top + half_rows, :]
            out_ref[:, lanes] = (
                dot(left_high, right_high) + dot(left_low, right_high) + dot(left_high, right_low)
            )


def cycle_part(layout, part, virt, occ, source, blocks, high, low):
    cols = blocks[0].shape[1]
    halves = cols // LANES
    rows, depth = high.shape
    wide = part * occ
    shape = jax.ShapeDtypeStruct((rows // 2, wide), F32)
    return pl.pallas_call(
        functools.partial(cycle_kernel, layout, part, occ),
        in_specs=[SMEM] + [VMEM] * len(blocks) + [VMEM, VMEM],
        out_specs=[VMEM, VMEM],
        out_shape=[shape, shape],
        scratch_shapes=[
            pltpu.VMEM((halves, virt * part, LANES), F32),
            pltpu.VMEM((depth, wide), BF16),
            pltpu.VMEM((depth, wide), BF16),
        ],
        compiler_params=params(18),
        cost_estimate=cost(6 * rows * depth * wide, 4 * virt * part * cols),
        name="cycle_part",
    )(source, *blocks, high, low)


def ladder_kernel(layout, part, q, again, source_ref, index_ref, *refs):
    count = len(layout)
    left_hbm = refs[count]
    before_ref = refs[count + 1] if again else None
    out_ref, left, held_high, held_low, right_high, right_low, sem = refs[count + 1 + again :]
    a_here, virt, _ = out_ref.shape
    slots = right_high.shape[1] // part
    groups = sem.shape[0]
    each = a_here // groups
    copies = [
        pltpu.make_async_copy(
            left_hbm.at[q, pl.ds(n * each, each)], left.at[pl.ds(n * each, each)], sem.at[n]
        )
        for n in range(groups)
    ]
    for copy in copies:
        copy.start()

    def store(start, rows, block):
        @pl.loop(0, rows // part)
        def _(c):
            there = pl.ds(pl.multiple_of(start + c * part, part), part)
            high, low = split(block[pl.ds(pl.multiple_of(c * part, part), part), :])
            held_high[there, :] = high
            held_low[there, :] = low

    place_blocks(layout, source_ref, refs[:count], store)

    for n in range(groups):
        copies[n].wait()

        for a in range(n * each, (n + 1) * each):
            turn = a % 2
            for s in range(slots):
                rows = pl.ds(pl.multiple_of(index_ref[a * slots + s] * part, part), part)
                right_high[turn, s * part : (s + 1) * part, :] = held_high[rows, :]
                right_low[turn, s * part : (s + 1) * part, :] = held_low[rows, :]
            both = dot(left[a], right_high[turn])
            total = both[:virt] + both[virt:] + dot(left[a, :virt], right_low[turn])
            if again:
                total = total + before_ref[a]
            out_ref[a] = total


def ladder_part(layout, part, q, source, index, blocks, left, before):
    cols = blocks[0].shape[1]
    _, a_here, rows, depth = left.shape
    virt = rows // 2
    again = before is not None
    return pl.pallas_call(
        functools.partial(ladder_kernel, layout, part, q, again),
        in_specs=[SMEM, SMEM] + [VMEM] * len(blocks) + [HBM] + [VMEM] * again,
        out_specs=VMEM,
        out_shape=jax.ShapeDtypeStruct((a_here, virt, cols), F32),
        scratch_shapes=[
            pltpu.VMEM((a_here, rows, depth), BF16),
            pltpu.VMEM((virt * part, cols), BF16),
            pltpu.VMEM((virt * part, cols), BF16),
            pltpu.VMEM((2, depth, cols), BF16),
            pltpu.VMEM((2, depth, cols), BF16),
            pltpu.SemaphoreType.DMA((4,)),
        ],
        input_output_aliases={3 + len(blocks): 0} if again else {},
        compiler_params=params(18),
        cost_estimate=cost(3 * a_here * rows * depth * cols, 2 * left.size // left.shape[0]),
        name="ladder_part",
    )(source, index, *blocks, left, *([before] if again else []))


def join_kernel(parts, part, occ, over, *refs):
    energies, terms = refs[:3], refs[3 : 3 + 3 * len(parts)]
    total_ref, out_ref, held = refs[3 + 3 * len(parts) :]
    energy_a, energy_b, energy_ij = energies
    a_here, virt, cols = total_ref.shape
    halves = cols // LANES
    per = LANES // occ

    @pl.loop(0, part // per)
    def _(g):
        lanes = pl.ds(pl.multiple_of(g * LANES, LANES), LANES)
        for n in range(len(parts)):
            keep_ref, near_ref, far_ref = terms[3 * n : 3 * n + 3]
            for h in range(halves):
                pieces = []
                for m in range(per):
                    here = pl.ds((h * per + m) * a_here, a_here)
                    pieces.append(
                        keep_ref[here, lanes] + near_ref[here, lanes] + far_ref[here, lanes]
                    )
                for m, piece in enumerate(swap_groups(pieces, occ)):
                    held[n, h, pl.ds(g * per + m, a_here, stride=part), :] = piece

    @pl.loop(0, a_here)
    def _(a):
        for q in range(virt // part):
            rows = slice(q * part, (q + 1) * part)
            total = total_ref[a, rows, :]
            if q in parts:
                n = parts.index(q)
                here = pl.ds(pl.multiple_of(a * part, part), part)
                total = total + jnp.concatenate([held[n, h, here, :] for h in range(halves)], axis=1)
            if q in over:
                low = (energy_a[pl.ds(a, 1), :] + energy_b[rows, :]) - energy_ij[...]
                total = total / low
            out_ref[a, rows, :] = total


def join(parts, part, occ, over, energies, terms, total):
    a_here, _, cols = total.shape
    return pl.pallas_call(
        functools.partial(join_kernel, parts, part, occ, over),
        in_specs=[VMEM] * (len(energies) + len(terms) + 1),
        out_specs=VMEM,
        out_shape=jax.ShapeDtypeStruct(total.shape, F32),
        scratch_shapes=[pltpu.VMEM((len(parts), cols // LANES, a_here * part, LANES), F32)],
        input_output_aliases={len(energies) + len(terms): 0},
        compiler_params=params(18),
        cost_estimate=cost(8 * a_here * part * cols, 20 * a_here * part * cols),
        name="join",
    )(*energies, *terms, total)


def ring_order(size):
    return list(range(0, size, 2)) + list(range(size - 1 - size % 2, 0, -2))


def per_device(
    amplitudes, ladder_blocks, ladder_index, cycle_blocks, cycle_index, eps_virt, eps_occ
):
    virt = eps_virt.shape[0]
    occ = eps_occ.shape[0]
    rows_here, cols = amplitudes.shape
    a_here = rows_here // virt
    i_here = cols // occ
    wide = lax.axis_size("wide")
    narrow = lax.axis_size("narrow")
    wide_pos = lax.axis_index("wide")
    narrow_pos = lax.axis_index("narrow")
    parts = PARTS
    part = virt // parts

    order = ring_order(wide)
    ahead = [(order[r], order[(r + 1) % wide]) for r in range(wide)]
    back = [(order[(r + 1) % wide], order[r]) for r in range(wide)]
    order_now = jnp.asarray(order, jnp.int32)
    spot = jnp.asarray([order.index(w) for w in range(wide)], jnp.int32)[wide_pos]
    steps = (wide - 1) // 2
    shifts = [0]
    for s in range(1, steps + 1):
        shifts += [-s, s]
    if wide % 2 == 0:
        shifts.append(wide // 2)
    source = order_now[(spot + jnp.asarray(shifts, jnp.int32)) % wide]

    own = amplitudes.reshape(a_here, virt, cols)
    rows_each = a_here * part

    hops = steps + (wide % 2 == 0)
    meet = hops // 2
    half = rows_each // 2
    layout = [(0, 0, rows_each)]
    for s in range(steps):
        layout += [(2 * s + 1, 0, rows_each), (2 * s + 2, 0, rows_each)]
    if wide % 2 == 0:
        layout += [(wide - 1, 0, half), (wide - 1, half, rows_each - half)]

    def tie(x, *others):
        return lax.optimization_barrier((x, *others))[0]

    ring = []
    for q in range(parts):
        whole = tie(own, ring[0][1]) if q else own
        block = whole[:, q * part : (q + 1) * part, :].reshape(rows_each, cols)
        ring.append([[block], block, block])

    token = []

    def ordered(x):
        return tie(x, *token) if token else x

    def hop(q, s, wait):
        blocks, right, left = ring[q]
        if wait:
            right, left, *_ = lax.optimization_barrier((right, left, *wait))
        if s == steps:
            right, left = right[:half], left[half:]
        right = lax.ppermute(right, "wide", ahead)
        left = lax.ppermute(left, "wide", back)
        blocks += [right, left]
        ring[q][1:] = [right, left]

    energy_a = lax.dynamic_slice_in_dim(eps_virt, wide_pos * a_here, a_here, 0)
    energy_i = lax.dynamic_slice_in_dim(eps_occ, narrow_pos * i_here, i_here, 0)
    energy_ij = (energy_i[:, None] + eps_occ[None, :]).reshape(1, cols)
    energies = [
        jnp.broadcast_to(energy_a[:, None], (a_here, cols)),
        jnp.broadcast_to(eps_virt[:, None], (virt, cols)),
        energy_ij,
    ]

    ladder_list = ladder_index.reshape(-1)
    keeps, nears, passes, fars = ([None] * parts for _ in range(4))
    total = None

    def cycle(q):
        blocks = [ordered(ring[q][0][0])] + ring[q][0][1:]
        keeps[q], send = cycle_part(layout, part, virt, occ, source, blocks, *dense)
        nears[q] = lax.ppermute(send, "narrow", [(n, n ^ 1) for n in range(narrow)])
        token[:] = [keeps[q]]

    def pass_on(q):
        keep = ordered(keeps[q])
        rows = keep.shape[0]
        passes[q] = keep[rows // 2 :] + nears[q][rows // 2 :]
        token[:] = [passes[q]]
        fars[q] = lax.ppermute(passes[q], "narrow", [(n, n ^ 2) for n in range(narrow)])

    def ladder(q, total):
        blocks = [ordered(ring[q][0][0])] + ring[q][0][1:]
        total = ladder_part(layout, part, q, source, ladder_list, blocks, split_left, total)
        token[:] = [total]
        return total

    def add(which, over, total):
        terms = [x for q in which for x in (keeps[q], nears[q], fars[q])]
        total = join(which, part, occ, over, energies, terms, ordered(total))
        token[:] = [total]
        return total

    def prepare(n, before):
        pieces = 4
        each = a_here // pieces
        out = ladder_prep(ordered(ladder_blocks), parts, n * each, each, before)
        token[:] = [out]
        return out

    walk = [[(0, s)] for s in range(meet)]
    for q in range(parts):
        rest = [(q, s) for s in range(meet, hops)]
        following = [(q + 1, s) for s in range(meet)] if q + 1 < parts else []
        for n in range(max(len(rest), len(following))):
            walk.append(rest[n : n + 1] + following[n : n + 1])
    whole_at = [max(n for n, step in enumerate(walk) if (q, hops - 1) in step) for q in range(parts)]

    last = parts - 1
    split_left = total = dense = None
    index_all = cycle_all = None
    place = narrow_pos.reshape(1).astype(jnp.int32)
    prepared = 0
    due = []
    for n, step in enumerate(walk):
        for q, s in step:
            hop(q, s, due)
        due = []
        if n == 0:
            index_all = lax.all_gather(cycle_index, "narrow", axis=0).reshape(-1)
            picked = lax.dynamic_slice_in_dim(
                tie(cycle_blocks, ring[0][0][0]), wide_pos * a_here, a_here, 2
            )
            cycle_all = lax.all_gather(picked, "narrow", axis=0)
        if prepared < 4:
            for _ in step:
                split_left = prepare(prepared, split_left)
                prepared += 1
        elif dense is None:
            dense = cycle_prep(place, ordered(index_all), cycle_all)
            token[:] = [dense[0]]
        for q in range(last):
            if n == whole_at[q] + 1:
                cycle(q)
            if n == whole_at[q] + 2:
                if q < last - 1:
                    total = ladder(q, total)
                pass_on(q)
            if n == whole_at[q] + 3:
                due.append(fars[q])
        due += token
    total = ladder(last - 1, total)
    token.append(fars[last - 1])
    cycle(last)
    pass_on(last)
    total = ladder(last, total)
    total = add(list(range(last)), list(range(last)), total)
    total = add([last], [last], total)
    return total.reshape(rows_here, cols)


def solution(mesh):
    in_specs = (
        P("wide", "narrow"),
        P("wide", None, None, None),
        P("wide", None),
        P(None, "narrow", None, None),
        P(None, "narrow"),
        P(),
        P(),
    )
    out_specs = P("wide", "narrow")
    return jax.shard_map(
        per_device, mesh=mesh, in_specs=in_specs, out_specs=out_specs, check_vma=False
    )
```

```python
import functools

import jax
import jax.numpy as jnp
from jax import lax
from jax.experimental import pallas as pl
from jax.experimental.pallas import tpu as pltpu
from jax.sharding import PartitionSpec as P

LANES = 128
PARTS = 4
VMEM_MIB = 64


def cost(flops, moved):
    return pl.CostEstimate(flops=flops // 1000, bytes_accessed=moved // 1000, transcendentals=0)

F32 = jnp.float32
BF16 = jnp.bfloat16
HBM = pl.BlockSpec(memory_space=pltpu.HBM)
VMEM = pl.BlockSpec(memory_space=pltpu.VMEM)
SMEM = pl.BlockSpec(memory_space=pltpu.SMEM)


def params(mib):
    return pltpu.CompilerParams(vmem_limit_bytes=mib << 20)


def split(x):
    high = x.astype(BF16)
    return high, (x - high.astype(F32)).astype(BF16)


def dot(x, y):
    return jnp.dot(x, y, preferred_element_type=F32)


def swap_groups(arrays, group):
    arrays = list(arrays)
    count = len(arrays)
    lane = lax.broadcasted_iota(jnp.int32, arrays[0].shape, 1) // group
    bit = 1
    while bit < count:
        odd = (lane & bit) != 0
        for low in range(count):
            if low & bit:
                continue
            high = low | bit
            up = pltpu.roll(arrays[high], bit * group, 1)
            down = pltpu.roll(arrays[low], LANES - bit * group, 1)
            arrays[low], arrays[high] = (
                jnp.where(odd, up, arrays[low]),
                jnp.where(odd, arrays[high], down),
            )
        bit *= 2
    return arrays


def ladder_prep_kernel(blocks_ref, *refs):
    out_ref = refs[-1]
    slots, virt, _ = blocks_ref.shape[1:]
    parts = out_ref.shape[0]
    part = virt // parts
    per = LANES // part
    for first in range(0, slots, per):
        pieces = [blocks_ref[0, first + s] for s in range(per)]
        for q, piece in enumerate(swap_groups(pieces, part)):
            high, low = split(piece)
            lanes = pl.ds(first * part, LANES)
            out_ref[q, 0, 0:virt, lanes] = high
            out_ref[q, 0, virt : 2 * virt, lanes] = low


def ladder_prep(blocks, parts, first, count, before):
    a_here, slots, virt, _ = blocks.shape
    depth = slots * (virt // parts)
    again = before is not None
    spare = -(-(VMEM_MIB << 20) // (parts * a_here * 2 * virt * depth * 2))
    return pl.pallas_call(
        ladder_prep_kernel,
        grid=(count,),
        in_specs=[pl.BlockSpec((1, slots, virt, virt), lambda a: (first + a, 0, 0, 0))] + [HBM] * again,
        out_specs=pl.BlockSpec((parts, 1, 2 * virt, depth), lambda a: (0, first + a, 0, 0)),
        out_shape=jax.ShapeDtypeStruct(((1 + spare) * parts, a_here, 2 * virt, depth), BF16),
        input_output_aliases={1: 0} if again else {},
        compiler_params=params(12),
        cost_estimate=cost(8 * blocks.size * count // a_here, 8 * blocks.size * count // a_here),
        name="ladder_prep",
    )(blocks, *([before] if again else []))


def mirrored(rel, size):
    out = 0
    bit = 1
    while bit < size:
        out = out * 2 + (rel // bit) % 2
        bit *= 2
    return out


def cycle_prep_kernel(place_ref, index_ref, blocks_ref, high_ref, low_ref, dense):
    shares, occ, slots, a_here, virt = blocks_ref.shape
    i_here = occ // shares
    mine = place_ref[0]
    dense[...] = jnp.zeros_like(dense)
    for owner in range(shares):
        rel = mine ^ owner
        base = mirrored(rel, shares) * i_here

        @pl.loop(0, i_here)
        def _(i):
            for share in range(shares):
                for s in range(slots):
                    row = (share * occ + owner * i_here + i) * slots + s
                    k = index_ref[row] - mine * i_here

                    @pl.when((k >= 0) & (k < i_here))
                    def _():
                        lanes = pl.ds(pl.multiple_of(k * virt, virt), virt)
                        dense[base + i, :, lanes] = blocks_ref[share, owner * i_here + i, s]

    rows = occ * a_here
    step = i_here * a_here
    for first in range(shares):
        piece = dense[first * i_here : (first + 1) * i_here].reshape(step, i_here * virt)
        high, low = split(piece)
        high_ref[first * step : (first + 1) * step, :] = high
        low_ref[first * step : (first + 1) * step, :] = low


def cycle_prep(place, index, blocks):
    shares, occ, slots, a_here, virt = blocks.shape
    shape = jax.ShapeDtypeStruct((occ * a_here, occ // shares * virt), BF16)
    return pl.pallas_call(
        cycle_prep_kernel,
        in_specs=[SMEM, SMEM, VMEM],
        out_specs=[VMEM, VMEM],
        out_shape=[shape, shape],
        scratch_shapes=[pltpu.VMEM((occ, a_here, occ // shares * virt), F32)],
        compiler_params=params(12),
        cost_estimate=cost(2 * blocks.size, 8 * blocks.size),
        name="cycle_prep",
    )(place, index, blocks)


def place_blocks(layout, source_ref, block_refs, store):
    rows_each = layout[0][2]
    for (owner, offset, rows), block in zip(layout, block_refs):
        store(pl.multiple_of(source_ref[owner] * rows_each + offset, rows), rows, block)


def cycle_kernel(layout, part, occ, source_ref, *refs):
    count = len(layout)
    high_ref, low_ref, keep_ref, send_ref, held, cols_high, cols_low = refs[count:]
    halves, rows, _ = held.shape
    virt = rows // part

    def store(start, rows, block):
        @pl.loop(0, rows // part)
        def _(c):
            here = pl.ds(pl.multiple_of(c * part, part), part)
            there = pl.ds(pl.multiple_of(start + c * part, part), part)
            for h in range(halves):
                held[h, there, :] = block[here, h * LANES : (h + 1) * LANES]

    place_blocks(layout, source_ref, refs[:count], store)
    per = LANES // occ
    half_rows = keep_ref.shape[0]
    width = 2 * LANES
    steps = part // per

    for first in range(0, steps, 2):
        for g in range(first, first + 2):
            for h in range(halves):
                pieces = [held[h, pl.ds(g * per + m, virt, stride=part), :] for m in range(per)]
                for m, piece in enumerate(swap_groups(pieces, occ)):
                    k = h * per + m
                    high, low = split(piece)
                    lanes = pl.ds(g * LANES, LANES)
                    cols_high[k * virt : (k + 1) * virt, lanes] = high
                    cols_low[k * virt : (k + 1) * virt, lanes] = low
        lanes = pl.ds(first * LANES, width)
        right_high = cols_high[:, lanes]
        right_low = cols_low[:, lanes]
        for out_ref, top in ((send_ref, half_rows), (keep_ref, 0)):
            left_high = high_ref[top : top + half_rows, :]
            left_low = low_ref[top : top + half_rows, :]
            out_ref[:, lanes] = (
                dot(left_high, right_high) + dot(left_low, right_high) + dot(left_high, right_low)
            )


def cycle_part(layout, part, virt, occ, source, blocks, high, low):
    cols = blocks[0].shape[1]
    halves = cols // LANES
    rows, depth = high.shape
    wide = part * occ
    shape = jax.ShapeDtypeStruct((rows // 2, wide), F32)
    return pl.pallas_call(
        functools.partial(cycle_kernel, layout, part, occ),
        in_specs=[SMEM] + [VMEM] * len(blocks) + [VMEM, VMEM],
        out_specs=[VMEM, VMEM],
        out_shape=[shape, shape],
        scratch_shapes=[
            pltpu.VMEM((halves, virt * part, LANES), F32),
            pltpu.VMEM((depth, wide), BF16),
            pltpu.VMEM((depth, wide), BF16),
        ],
        compiler_params=params(18),
        cost_estimate=cost(6 * rows * depth * wide, 4 * virt * part * cols),
        name="cycle_part",
    )(source, *blocks, high, low)


def ladder_kernel(layout, part, q, again, last, source_ref, index_ref, *refs):
    count = len(layout)
    left_hbm = refs[count]
    before_ref = refs[count + 1] if again else None
    energies = refs[count + 1 + again : count + 1 + again + 3 * last]
    out_ref, left, held_high, held_low, right_high, right_low, sem = refs[
        count + 1 + again + 3 * last :
    ]
    a_here, virt, _ = out_ref.shape
    slots = right_high.shape[1] // part
    groups = sem.shape[0]
    each = a_here // groups
    copies = [
        pltpu.make_async_copy(
            left_hbm.at[q, pl.ds(n * each, each)], left.at[pl.ds(n * each, each)], sem.at[n]
        )
        for n in range(groups)
    ]
    for copy in copies:
        copy.start()

    def store(start, rows, block):
        @pl.loop(0, rows // part)
        def _(c):
            there = pl.ds(pl.multiple_of(start + c * part, part), part)
            high, low = split(block[pl.ds(pl.multiple_of(c * part, part), part), :])
            held_high[there, :] = high
            held_low[there, :] = low

    place_blocks(layout, source_ref, refs[:count], store)

    for n in range(groups):
        copies[n].wait()

        for a in range(n * each, (n + 1) * each):
            turn = a % 2
            for s in range(slots):
                rows = pl.ds(pl.multiple_of(index_ref[a * slots + s] * part, part), part)
                right_high[turn, s * part : (s + 1) * part, :] = held_high[rows, :]
                right_low[turn, s * part : (s + 1) * part, :] = held_low[rows, :]
            both = dot(left[a], right_high[turn])
            total = both[:virt] + both[virt:] + dot(left[a, :virt], right_low[turn])
            if again:
                total = total + before_ref[a]
            if last:
                energy_a, energy_b, energy_ij = energies
                low = (energy_a[pl.ds(a, 1), :] + energy_b[...]) - energy_ij[...]
                row = lax.broadcasted_iota(jnp.int32, total.shape, 0)
                total = jnp.where(row < virt - part, total / low, total)
            out_ref[a] = total


def ladder_part(layout, part, q, source, index, blocks, left, before, energies):
    cols = blocks[0].shape[1]
    _, a_here, rows, depth = left.shape
    virt = rows // 2
    again = before is not None
    last = len(energies) > 0
    return pl.pallas_call(
        functools.partial(ladder_kernel, layout, part, q, again, last),
        in_specs=[SMEM, SMEM] + [VMEM] * len(blocks) + [HBM] + [VMEM] * (again + len(energies)),
        out_specs=VMEM,
        out_shape=jax.ShapeDtypeStruct((a_here, virt, cols), F32),
        scratch_shapes=[
            pltpu.VMEM((a_here, rows, depth), BF16),
            pltpu.VMEM((virt * part, cols), BF16),
            pltpu.VMEM((virt * part, cols), BF16),
            pltpu.VMEM((2, depth, cols), BF16),
            pltpu.VMEM((2, depth, cols), BF16),
            pltpu.SemaphoreType.DMA((4,)),
        ],
        input_output_aliases={3 + len(blocks): 0} if again else {},
        compiler_params=params(18),
        cost_estimate=cost(3 * a_here * rows * depth * cols, 2 * left.size // left.shape[0]),
        name="ladder_part",
    )(source, index, *blocks, left, *([before] if again else []), *energies)


def join_kernel(q, part, occ, last, *refs):
    energy_a, energy_b, energy_ij, keep_ref, near_ref, far_ref, total_ref, out_ref, held = refs
    a_here, virt, cols = total_ref.shape
    halves = cols // LANES
    per = LANES // occ

    @pl.loop(0, part // per)
    def _(g):
        lanes = pl.ds(pl.multiple_of(g * LANES, LANES), LANES)
        for h in range(halves):
            pieces = []
            for m in range(per):
                here = pl.ds((h * per + m) * a_here, a_here)
                pieces.append(keep_ref[here, lanes] + near_ref[here, lanes] + far_ref[here, lanes])
            for m, piece in enumerate(swap_groups(pieces, occ)):
                held[h, pl.ds(g * per + m, a_here, stride=part), :] = piece

    @pl.loop(0, a_here)
    def _(a):
        for first in range(0, virt, part):
            rows = slice(first, first + part)
            total = total_ref[a, rows, :]
            if first == q * part:
                here = pl.ds(pl.multiple_of(a * part, part), part)
                total = total + jnp.concatenate([held[h, here, :] for h in range(halves)], axis=1)
                if last:
                    low = (energy_a[pl.ds(a, 1), :] + energy_b[rows, :]) - energy_ij[...]
                    total = total / low
            out_ref[a, rows, :] = total


def join(q, part, occ, last, energies, keep, near, far, total):
    a_here, _, cols = total.shape
    return pl.pallas_call(
        functools.partial(join_kernel, q, part, occ, last),
        in_specs=[VMEM] * (len(energies) + 4),
        out_specs=VMEM,
        out_shape=jax.ShapeDtypeStruct(total.shape, F32),
        scratch_shapes=[pltpu.VMEM((cols // LANES, a_here * part, LANES), F32)],
        input_output_aliases={len(energies) + 3: 0},
        compiler_params=params(18),
        cost_estimate=cost(8 * a_here * part * cols, 20 * a_here * part * cols),
        name="join",
    )(*energies, keep, near, far, total)


def ring_order(size):
    return list(range(0, size, 2)) + list(range(size - 1 - size % 2, 0, -2))


def per_device(
    amplitudes, ladder_blocks, ladder_index, cycle_blocks, cycle_index, eps_virt, eps_occ
):
    virt = eps_virt.shape[0]
    occ = eps_occ.shape[0]
    rows_here, cols = amplitudes.shape
    a_here = rows_here // virt
    i_here = cols // occ
    wide = lax.axis_size("wide")
    narrow = lax.axis_size("narrow")
    wide_pos = lax.axis_index("wide")
    narrow_pos = lax.axis_index("narrow")
    parts = PARTS
    part = virt // parts

    order = ring_order(wide)
    ahead = [(order[r], order[(r + 1) % wide]) for r in range(wide)]
    back = [(order[(r + 1) % wide], order[r]) for r in range(wide)]
    order_now = jnp.asarray(order, jnp.int32)
    spot = jnp.asarray([order.index(w) for w in range(wide)], jnp.int32)[wide_pos]
    steps = (wide - 1) // 2
    shifts = [0]
    for s in range(1, steps + 1):
        shifts += [-s, s]
    if wide % 2 == 0:
        shifts.append(wide // 2)
    source = order_now[(spot + jnp.asarray(shifts, jnp.int32)) % wide]

    own = amplitudes.reshape(a_here, virt, cols)
    rows_each = a_here * part

    hops = steps + (wide % 2 == 0)
    meet = hops // 2
    half = rows_each // 2
    layout = [(0, 0, rows_each)]
    for s in range(steps):
        layout += [(2 * s + 1, 0, rows_each), (2 * s + 2, 0, rows_each)]
    if wide % 2 == 0:
        layout += [(wide - 1, 0, half), (wide - 1, half, rows_each - half)]

    def tie(x, *others):
        return lax.optimization_barrier((x, *others))[0]

    ring = []
    for q in range(parts):
        whole = tie(own, ring[0][1]) if q else own
        block = whole[:, q * part : (q + 1) * part, :].reshape(rows_each, cols)
        ring.append([[block], block, block])

    token = []

    def ordered(x):
        return tie(x, *token) if token else x

    def hop(q, s, wait):
        blocks, right, left = ring[q]
        if wait:
            right, left, *_ = lax.optimization_barrier((right, left, *wait))
        if s == steps:
            right, left = right[:half], left[half:]
        right = lax.ppermute(right, "wide", ahead)
        left = lax.ppermute(left, "wide", back)
        blocks += [right, left]
        ring[q][1:] = [right, left]

    energy_a = lax.dynamic_slice_in_dim(eps_virt, wide_pos * a_here, a_here, 0)
    energy_i = lax.dynamic_slice_in_dim(eps_occ, narrow_pos * i_here, i_here, 0)
    energy_ij = (energy_i[:, None] + eps_occ[None, :]).reshape(1, cols)
    energies = [
        jnp.broadcast_to(energy_a[:, None], (a_here, cols)),
        jnp.broadcast_to(eps_virt[:, None], (virt, cols)),
        energy_ij,
    ]

    ladder_list = ladder_index.reshape(-1)
    keeps, nears, passes, fars = ([None] * parts for _ in range(4))
    total = None

    def cycle(q):
        blocks = [ordered(ring[q][0][0])] + ring[q][0][1:]
        keeps[q], send = cycle_part(layout, part, virt, occ, source, blocks, *dense)
        nears[q] = lax.ppermute(send, "narrow", [(n, n ^ 1) for n in range(narrow)])
        token[:] = [keeps[q]]

    def pass_on(q):
        keep = ordered(keeps[q])
        rows = keep.shape[0]
        passes[q] = keep[rows // 2 :] + nears[q][rows // 2 :]
        token[:] = [passes[q]]
        fars[q] = lax.ppermute(passes[q], "narrow", [(n, n ^ 2) for n in range(narrow)])

    def ladder(q, total):
        blocks = [ordered(ring[q][0][0])] + ring[q][0][1:]
        final = energies if q == parts - 1 else []
        total = ladder_part(
            layout, part, q, source, ladder_list, blocks, split_left, total, final
        )
        token[:] = [total]
        return total

    def add(q, total):
        last = q == parts - 1
        total = join(
            q, part, occ, last, energies, keeps[q], nears[q], fars[q], ordered(total)
        )
        token[:] = [total]
        return total

    def prepare(n, before):
        pieces = 4
        each = a_here // pieces
        out = ladder_prep(ordered(ladder_blocks), parts, n * each, each, before)
        token[:] = [out]
        return out

    walk = [[(0, s)] for s in range(meet)]
    for q in range(parts):
        rest = [(q, s) for s in range(meet, hops)]
        following = [(q + 1, s) for s in range(meet)] if q + 1 < parts else []
        for n in range(max(len(rest), len(following))):
            walk.append(rest[n : n + 1] + following[n : n + 1])
    whole_at = [max(n for n, step in enumerate(walk) if (q, hops - 1) in step) for q in range(parts)]

    last = parts - 1
    split_left = total = dense = None
    index_all = cycle_all = None
    place = narrow_pos.reshape(1).astype(jnp.int32)
    prepared = 0
    due = []
    for n, step in enumerate(walk):
        for q, s in step:
            hop(q, s, due)
        due = []
        if n == 0:
            index_all = lax.all_gather(cycle_index, "narrow", axis=0).reshape(-1)
            picked = lax.dynamic_slice_in_dim(
                tie(cycle_blocks, ring[0][0][0]), wide_pos * a_here, a_here, 2
            )
            cycle_all = lax.all_gather(picked, "narrow", axis=0)
        if prepared < 4:
            for _ in step:
                split_left = prepare(prepared, split_left)
                prepared += 1
        elif dense is None:
            dense = cycle_prep(place, ordered(index_all), cycle_all)
            token[:] = [dense[0]]
        for q in range(last):
            if n == whole_at[q] + 1:
                cycle(q)
            if n == whole_at[q] + 2:
                if q < last - 1:
                    total = ladder(q, total)
                pass_on(q)
            if n == whole_at[q] + 3:
                due.append(fars[q])
        due += token
    total = ladder(last - 1, total)
    cycle(last)
    for q in range(last - 1):
        total = add(q, total)
    token.append(fars[last - 1])
    pass_on(last)
    total = add(last - 1, total)
    total = ladder(last, total)
    total = add(last, total)
    return total.reshape(rows_here, cols)


def solution(mesh):
    in_specs = (
        P("wide", "narrow"),
        P("wide", None, None, None),
        P("wide", None),
        P(None, "narrow", None, None),
        P(None, "narrow"),
        P(),
        P(),
    )
    out_specs = P("wide", "narrow")
    return jax.shard_map(
        per_device, mesh=mesh, in_specs=in_specs, out_specs=out_specs, check_vma=False
    )
```
